512 devices in a mesh: seq: 16 (over y, core), grp: 32 (over z, x).
Axes of the slice: x: 4, y: 8, z: 8, core: 2. Of those that a mesh axis runs over, the one named last changes fastest.
Arguments:
- queries: bfloat16 [65536, 1024], P(('seq', 'grp')), as said below
- key_rows: bfloat16 [65536, 1024], P(('seq', 'grp')), as said below
- value_rows: bfloat16 [65536, 1024], P(('seq', 'grp')), may hold values from -6 to 6
- cotangent: bfloat16 [65536, 1024], P(('seq', 'grp')), may hold values from -6 to 6
- out_weight: bfloat16 [1024, 1024], replicated, may hold values from -0.1875 to 0.1875
- send_lists: int32 [32, 32, 1], P('grp'), may hold values from 0 to 15
- key_blocks: int32 [32, 16, 8], P('grp'), may hold values from 0 to 47, as said below
- key_counts: int32 [32, 16], P('grp'), may hold values from 1 to 8, as said below
Outputs:
- layer_out: bfloat16 [65536, 1024], P(('seq', 'grp'))
- query_grad: bfloat16 [65536, 1024], P(('seq', 'grp'))
- key_grad: bfloat16 [65536, 1024], P(('seq', 'grp'))
- value_grad: bfloat16 [65536, 1024], P(('seq', 'grp'))
- weight_grad: float32 [1024, 1024], P('grp')
The draws below stay inside these ranges and needn't reach their ends.
Inputs may be any that keep to these rules, and one draw needn't show every extreme that they name: `queries`: entries within -6 to 6. `key_rows`: entries within -6 to 6. `key_blocks`: the first listed block of query block b of a group is block b of that group itself; entries at t >= the block's count are unused. `key_counts`: every group has a query block with all 8 listed blocks live.
All inputs are finite; a program needn't handle non-finite values.
Results may differ from the reference program's by a relative error of at most 0.015.
Values may be sent and summed in bfloat16 or wider, within the bound.
A program may use at most 64 MiB of HBM per device.

```python
import math
import jax
import jax.numpy as jnp
from jax import lax

D = 1024
HEADS = 16
HD = 64
BLOCK = 128
RB = 1
KB = 8
MAXB = 1
ROWS = 128
NBG = 16
NE = 48
NODES = 65536
N_SEQ = 16
N_GRP = 32


def draw_queries(key, part):
    key = jax.random.fold_in(key, 101)
    values = jnp.clip(jax.random.normal(key, (NODES, D), jnp.float32), -6.0, 6.0)
    return values.astype(jnp.bfloat16)


def draw_key_rows(key, part):
    key = jax.random.fold_in(key, 202)
    values = jnp.clip(jax.random.normal(key, (NODES, D), jnp.float32), -6.0, 6.0)
    return values.astype(jnp.bfloat16)


def draw_key_blocks(key, part):
    key = jax.random.fold_in(key, 303)
    picks = jax.random.randint(key, (N_GRP, NBG, KB), 0, NE, dtype=jnp.int32)
    own = jnp.arange(NBG, dtype=jnp.int32)
    return picks.at[:, :, 0].set(jnp.broadcast_to(own[None, :], (N_GRP, NBG)))


def draw_key_counts(key, part):
    key = jax.random.fold_in(key, 404)
    first_key, second_key = jax.random.split(key)
    counts = jax.random.randint(first_key, (N_GRP, NBG), 1, KB + 1, dtype=jnp.int32)
    where_full = jax.random.randint(second_key, (N_GRP,), 0, NBG, dtype=jnp.int32)
    full_mask = jnp.arange(NBG, dtype=jnp.int32)[None, :] == where_full[:, None]
    return jnp.where(full_mask, KB, counts).astype(jnp.int32)


def place_ends(drawn, rng, smallest, top_value):
    index_at = [jax.random.randint(jax.random.fold_in(rng, axis), (), 0, length) for axis, length in enumerate(drawn.shape)]
    longest = drawn.shape.index(max(drawn.shape))
    next_to = index_at[:longest] + [(index_at[longest] + 1) % drawn.shape[longest]] + index_at[longest + 1:]
    return drawn.at[tuple(index_at)].set(smallest).at[tuple(next_to)].set(top_value)


def levels(rng, shape, cuts, least, largest):
    def one(dim, shards_of):
        steps = jax.random.uniform(jax.random.fold_in(jax.random.fold_in(rng, 6), dim), (shards_of,), jnp.float32, least / len(cuts), largest / len(cuts))
        return jnp.repeat(jnp.exp(steps), shape[dim] // shards_of).reshape((-1,) + (1,) * (len(shape) - dim - 1))

    gain = one(*cuts[0])
    for cut in cuts[1:]:
        gain = gain * one(*cut)
    return gain


def scatter_about(rng, dims, scale, limit, cuts=(), kind=jnp.bfloat16):
    gain = levels(rng, dims, cuts, -0.22, 0.18) if cuts else 1.0
    result = jax.random.normal(rng, dims, jnp.float32) * scale * gain
    return jnp.minimum(jnp.maximum(result, -limit), limit).astype(kind)


def setup_inputs(seed: int = 0) -> dict:
    splits = jax.random.split(jax.random.key(seed), 9)
    queries = draw_queries(jax.random.fold_in(splits[8], 71), 0)
    key_rows = draw_key_rows(jax.random.fold_in(splits[8], 71), 0)
    value_rows = scatter_about(splits[2], (NODES, D), 1.0, 6.0, ((0, 512),))
    cotangent = scatter_about(splits[3], (NODES, D), 1.0, 6.0, ((0, 512),))
    out_weight = scatter_about(splits[4], (D, D), D ** -0.5, 0.1875)
    send_lists = place_ends(jax.random.randint(splits[5], (N_GRP, N_GRP, MAXB), 0, NBG), jax.random.fold_in(splits[5], 1), 0, NBG - 1).astype(jnp.int32)
    key_blocks = draw_key_blocks(jax.random.fold_in(splits[8], 71), 0)
    key_counts = draw_key_counts(jax.random.fold_in(splits[8], 71), 0)
    return {"queries": queries, "key_rows": key_rows, "value_rows": value_rows, "cotangent": cotangent, "out_weight": out_weight, "send_lists": send_lists, "key_blocks": key_blocks, "key_counts": key_counts}


def span_step(query_blk, extended, list_rows, counts, grad_blk, score_scale):
    chosen = extended[list_rows]
    listed_shape = chosen.shape
    key_width = listed_shape[1] * listed_shape[2]
    chosen = chosen.reshape(listed_shape[0], key_width, 2, listed_shape[4], listed_shape[5])
    key_part = chosen[:, :, 0].astype(jnp.float32)
    value_part = chosen[:, :, 1].astype(jnp.float32)
    query_full = query_blk.astype(jnp.float32)
    grad_full = grad_blk.astype(jnp.float32)
    scores = jnp.einsum('cihe,cjhe->chij', query_full, key_part) * score_scale
    column = jnp.arange(key_width, dtype=jnp.int32) // listed_shape[2]
    live_mask = column[None, :] < counts[:, None]
    scores = jnp.where(live_mask[:, None, None, :], scores, -jnp.inf)
    row_top = lax.optimization_barrier(jnp.max(scores, axis=-1, keepdims=True))
    weights = jnp.exp(scores - row_top)
    prob_full = weights / lax.optimization_barrier(jnp.sum(weights, axis=-1, keepdims=True))
    probs_low = prob_full.astype(jnp.bfloat16)
    attended = jnp.einsum('chij,cjhe->cihe', probs_low.astype(jnp.float32), value_part).astype(jnp.bfloat16)
    dprobs = jnp.einsum('cihe,cjhe->chij', grad_full, value_part)
    row_inner = lax.optimization_barrier(jnp.sum(prob_full * dprobs, axis=-1, keepdims=True))
    dscores = (prob_full * (dprobs - row_inner) * score_scale).astype(jnp.bfloat16)
    dquery = jnp.einsum('chij,cjhe->cihe', dscores.astype(jnp.float32), key_part).astype(jnp.bfloat16)
    key_grad = jnp.einsum('chij,cihe->cjhe', dscores.astype(jnp.float32), query_full)
    dvalue = jnp.einsum('chij,cihe->cjhe', probs_low.astype(jnp.float32), grad_full)
    pair_grad = jnp.stack((key_grad, dvalue), axis=2).reshape(listed_shape)
    return (attended, dquery, pair_grad)

def group_pass(query_rows, extended, list_rows, counts, grad_rows):
    group_blocks = list_rows.shape[0]
    block_rows = extended.shape[1]
    head_count = query_rows.shape[1]
    head_size = query_rows.shape[2]
    group_size = math.gcd(group_blocks, max(1, 512 // block_rows))
    steps_count = group_blocks // group_size
    score_scale = 1.0 / math.sqrt(head_size)
    query_steps = query_rows.reshape(steps_count, group_size, block_rows, head_count, head_size)
    grad_steps = grad_rows.reshape(steps_count, group_size, block_rows, head_count, head_size)
    list_steps = list_rows.reshape(steps_count, group_size, list_rows.shape[1])
    count_steps = counts.reshape(steps_count, group_size)

    def advance(grad_total, pieces):
        query_blk, list_blk, count_blk, grad_blk = pieces
        attended, dquery, pair_grad = span_step(query_blk, extended, list_blk, count_blk, grad_blk, score_scale)
        grad_total = grad_total.at[list_blk].add(pair_grad)
        return (grad_total, (attended, dquery))
    start_total = jnp.zeros(extended.shape, jnp.float32)
    grad_total, outputs = lax.scan(advance, start_total, (query_steps, list_steps, count_steps, grad_steps))
    attended = outputs[0].reshape(group_blocks * block_rows, head_count, head_size)
    dquery = outputs[1].reshape(group_blocks * block_rows, head_count, head_size)
    return (attended, dquery, grad_total)

def reference(queries, key_rows, value_rows, cotangent, out_weight, send_lists, key_blocks, key_counts):
    group_blocks = RB * N_SEQ

    def by_group(rows_in):
        shaped = rows_in.reshape(N_SEQ, N_GRP, ROWS, D).transpose(1, 0, 2, 3)
        return shaped.reshape(N_GRP, group_blocks, BLOCK, HEADS, HD)

    def to_nodes(grouped):
        shaped = grouped.reshape(N_GRP, N_SEQ, ROWS, D).transpose(1, 0, 2, 3)
        return shaped.reshape(NODES, D)
    incoming_grad = jnp.dot(cotangent, out_weight.T, preferred_element_type=jnp.float32).astype(jnp.bfloat16)
    query_groups = by_group(queries)
    grad_groups = by_group(incoming_grad)
    pair_all = jnp.stack((by_group(key_rows), by_group(value_rows)), axis=3)
    sources = jnp.arange(N_GRP, dtype=jnp.int32)[:, None]

    def one_group(grad_sum, group_index):
        picked = send_lists[:, group_index, :]
        halo_rows = pair_all[sources, picked].reshape(N_GRP * MAXB, BLOCK, 2, HEADS, HD)
        extended = jnp.concatenate((pair_all[group_index], halo_rows), axis=0)
        query_rows = query_groups[group_index].reshape(group_blocks * BLOCK, HEADS, HD)
        grad_rows = grad_groups[group_index].reshape(group_blocks * BLOCK, HEADS, HD)
        attended, dquery, grad_total = group_pass(query_rows, extended, key_blocks[group_index], key_counts[group_index], grad_rows)
        grad_sum = grad_sum.at[group_index].add(grad_total[:group_blocks])
        returned = grad_total[group_blocks:].reshape(N_GRP, MAXB, BLOCK, 2, HEADS, HD)
        grad_sum = grad_sum.at[sources, picked].add(returned)
        return (grad_sum, (attended, dquery))
    start_sum = jnp.zeros(pair_all.shape, jnp.float32)
    grad_sum, outputs = lax.scan(one_group, start_sum, jnp.arange(N_GRP, dtype=jnp.int32))
    attended = to_nodes(outputs[0])
    query_grad = to_nodes(outputs[1])
    grad_low = grad_sum.astype(jnp.bfloat16)
    key_grad = to_nodes(grad_low[:, :, :, 0])
    value_grad = to_nodes(grad_low[:, :, :, 1])
    layer_out = jnp.dot(attended, out_weight, preferred_element_type=jnp.float32).astype(jnp.bfloat16)
    inverse_root = 1.0 / math.sqrt(float(NODES))
    weight_grad = jnp.dot(attended.T, cotangent, preferred_element_type=jnp.float32) * inverse_root
    return (layer_out, query_grad, key_grad, value_grad, weight_grad)
```

```python
import functools
import math

import jax
import jax.numpy as jnp
from jax import lax
from jax.experimental import pallas as pl
from jax.experimental.pallas import tpu as pltpu
from jax.sharding import PartitionSpec as P

HD = 64
LANES = 128
BF = jnp.bfloat16
F32 = jnp.float32
VMEM = pl.BlockSpec(memory_space=pltpu.VMEM)
SMEM = pl.BlockSpec(memory_space=pltpu.SMEM)
LIMIT = 48 * 1024 * 1024


def weave(left, right):
    lane = lax.broadcasted_iota(jnp.int32, left.shape, 1)
    left_f, right_f = left.astype(F32), right.astype(F32)
    first = jnp.where(lane < HD, left_f, pltpu.roll(right_f, HD, 1))
    second = jnp.where(lane < HD, pltpu.roll(left_f, HD, 1), right_f)
    return first, second


def pack_kernel(q_ref, k_ref, v_ref, c_ref, w_ref, kv_ref, qg_ref):
    grad = lax.dot_general(
        c_ref[...], w_ref[...], (((1,), (1,)), ((), ())), preferred_element_type=F32
    ).astype(BF)
    for j in range(kv_ref.shape[0] // 2):
        cols = slice(j * LANES, (j + 1) * LANES)
        first, second = weave(k_ref[:, cols], v_ref[:, cols])
        kv_ref[2 * j] = first.astype(BF)
        kv_ref[2 * j + 1] = second.astype(BF)
        first, second = weave(q_ref[:, cols], grad[:, cols])
        qg_ref[2 * j] = first.astype(BF)
        qg_ref[2 * j + 1] = second.astype(BF)


def attend_kernel(
    list_ref, count_ref, qg_ref, kv_ref, cot_ref, aq_ref, own_ref, halo_ref, term_ref, kv_t, acc, att_t
):
    blocks, rows, _ = qg_ref.shape
    space = kv_ref.shape[0]
    listed = list_ref.shape[1]
    scale = 1.0 / math.sqrt(HD)

    def prepare(i, carry):
        kv_t[i] = kv_ref[i].T
        acc[i] = jnp.zeros(acc.shape[1:], F32)
        return carry

    lax.fori_loop(0, space, prepare, 0, unroll=4)

    def one(b, live):
        qg = qg_ref[b]
        lane = lax.broadcasted_iota(jnp.int32, qg.shape, 1)
        full = qg.astype(F32)
        x = jnp.concatenate(
            (
                jnp.where(lane < HD, full * scale, 0.0).astype(BF),
                jnp.where(lane < HD, 0.0, full).astype(BF),
            ),
            axis=0,
        )
        index = [list_ref[b, t] for t in range(live)]
        keys = jnp.concatenate([kv_ref[i] for i in index], axis=0)
        both = lax.dot_general(keys, x, (((1,), (1,)), ((), ())), preferred_element_type=F32)
        scores, dprobs = both[:, :rows], both[:, rows:]
        weights = jnp.exp(scores - jnp.max(scores, axis=0, keepdims=True))
        inverse = 1.0 / jnp.sum(weights, axis=0, keepdims=True)
        probs = weights * inverse
        inner = jnp.sum(probs * dprobs, axis=0, keepdims=True)
        z = jnp.concatenate((probs * (dprobs - inner), probs), axis=1).astype(BF)
        pair = jnp.dot(z, x, preferred_element_type=F32)
        for t, i in enumerate(index):
            acc[i] += pair[t * rows : (t + 1) * rows]
        turned = jnp.concatenate([kv_t[i] for i in index], axis=1)
        out = jnp.dot(turned, z, preferred_element_type=F32)
        attended = out[HD:, rows:]
        att_t[:, pl.ds(pl.multiple_of(b * rows, rows), rows)] = attended.astype(BF)
        aq_ref[b] = jnp.concatenate((out[:HD, :rows] * scale, attended), axis=0).T.astype(BF)

    def step(b, carry):
        count = count_ref[0, b]
        for live in range(1, listed + 1):
            pl.when(count == live)(functools.partial(one, b, live))
        return carry

    lax.fori_loop(0, blocks, step, 0)
    own_ref[...] = acc[:blocks]
    halo_ref[...] = acc[blocks:].astype(BF)
    term_ref[...] = jnp.dot(att_t[...], cot_ref[...], preferred_element_type=F32)


def settle_kernel(send_ref, own_ref, back_ref, out_ref, acc):
    acc[...] = own_ref[...]

    def add(g, carry):
        i = send_ref[0, g]
        acc[i] += back_ref[g].astype(F32)
        return carry

    lax.fori_loop(0, back_ref.shape[0], add, 0, unroll=4)
    out_ref[...] = acc[...].astype(BF)


def unpack_kernel(aq_ref, kv_ref, w_ref, out_ref, dq_ref, dk_ref, dv_ref, att):
    for j in range(aq_ref.shape[0] // 2):
        cols = slice(j * LANES, (j + 1) * LANES)
        first, second = weave(aq_ref[2 * j], aq_ref[2 * j + 1])
        dq_ref[:, cols] = first.astype(BF)
        att[:, cols] = second.astype(BF)
        first, second = weave(kv_ref[2 * j], kv_ref[2 * j + 1])
        dk_ref[:, cols] = first.astype(BF)
        dv_ref[:, cols] = second.astype(BF)
    out_ref[...] = jnp.dot(att[...], w_ref[...], preferred_element_type=F32).astype(BF)


def shape(dims, kind=BF):
    return jax.ShapeDtypeStruct(dims, kind)


def call(kernel, in_specs, out_shape, scratch=(), **kw):
    return pl.pallas_call(
        kernel,
        in_specs=in_specs,
        out_specs=jax.tree.map(lambda _: VMEM, out_shape),
        out_shape=out_shape,
        scratch_shapes=list(scratch),
        compiler_params=pltpu.CompilerParams(vmem_limit_bytes=LIMIT),
        **kw,
    )


def attend(lists, counts, qg, kv, cot):
    blocks, rows, lanes = qg.shape
    space = kv.shape[0]
    return call(
        attend_kernel,
        [SMEM, SMEM, VMEM, VMEM, VMEM],
        (
            shape((blocks, rows, lanes)),
            shape((blocks, rows, lanes), F32),
            shape((space - blocks, rows, lanes)),
            shape((HD, cot.shape[1]), F32),
        ),
        [
            pltpu.VMEM((space, lanes, rows), BF),
            pltpu.VMEM((space, rows, lanes), F32),
            pltpu.VMEM((HD, blocks * rows), BF),
        ],
    )(lists, counts, qg, kv, cot)


def per_device(
    queries, key_rows, value_rows, cotangent, out_weight, send_lists, key_blocks, key_counts
):
    seq_count = lax.axis_size("seq")
    grp_count = lax.axis_size("grp")
    rows, width = queries.shape
    heads = width // HD
    packed = shape((heads, rows, 2 * HD))
    kv, qg = call(pack_kernel, [VMEM] * 5, (packed, packed))(
        queries, key_rows, value_rows, cotangent, out_weight
    )
    kv = lax.all_to_all(kv, "seq", split_axis=0, concat_axis=0, tiled=True)
    qg = lax.all_to_all(qg, "seq", split_axis=0, concat_axis=0, tiled=True)
    halo = lax.all_to_all(
        kv[send_lists[0, :, 0]], "grp", split_axis=0, concat_axis=0, tiled=True
    )
    cot = lax.all_gather(cotangent, "seq", axis=0, tiled=True)
    aq, own, halo, term = attend(
        key_blocks[0], key_counts, qg, jnp.concatenate((kv, halo), axis=0), cot
    )
    aq = lax.all_to_all(aq, "seq", split_axis=0, concat_axis=0, tiled=True)
    back = lax.all_to_all(halo, "grp", split_axis=0, concat_axis=0, tiled=True)
    inverse_root = 1.0 / math.sqrt(float(rows * seq_count * grp_count))
    part = lax.psum_scatter(term * inverse_root, "grp", scatter_dimension=0, tiled=True)
    part = lax.all_gather(part, "seq", axis=0, tiled=False)
    per_group = width // grp_count
    wanted = jnp.arange(grp_count)
    mine = lax.axis_index("grp")
    span = HD // per_group
    outgoing = jnp.where(
        (mine // (grp_count // span) == wanted % span)[:, None, None], part[wanted // span], 0.0
    )
    incoming = lax.all_to_all(outgoing, "grp", split_axis=0, concat_axis=0, tiled=True)
    weight_grad = lax.dynamic_slice_in_dim(
        incoming, (mine % span) * (grp_count // span), grp_count // span, 0
    ).reshape(per_group, width)

    dkv = call(settle_kernel, [SMEM, VMEM, VMEM], shape(own.shape), [pltpu.VMEM(own.shape, F32)])(
        send_lists[:, :, 0], own, back
    )
    dkv = lax.all_to_all(dkv, "seq", split_axis=0, concat_axis=0, tiled=True)
    flat = shape((rows, width))
    layer_out, dq, dk, dv = call(
        unpack_kernel, [VMEM] * 3, (flat,) * 4, [pltpu.VMEM((rows, width), BF)]
    )(aq, dkv, out_weight)
    return layer_out, dq, dk, dv, weight_grad


def solution(mesh):
    nodes = P(("seq", "grp"), None)
    by_group = P("grp", None, None)
    return jax.shard_map(
        per_device,
        mesh=mesh,
        in_specs=(nodes, nodes, nodes, nodes, P(), by_group, by_group, P("grp", None)),
        out_specs=(nodes, nodes, nodes, nodes, P("grp", None)),
        check_vma=False,
    )
```

```python
import functools
import math

import jax
import jax.numpy as jnp
from jax import lax
from jax.experimental import pallas as pl
from jax.experimental.pallas import tpu as pltpu
from jax.sharding import PartitionSpec as P

HD = 64
LANES = 128
BF = jnp.bfloat16
F32 = jnp.float32
VMEM = pl.BlockSpec(memory_space=pltpu.VMEM)
SMEM = pl.BlockSpec(memory_space=pltpu.SMEM)
LIMIT = 48 * 1024 * 1024
MESH = pl.DeviceIdType.MESH


def weave(left, right):
    lane = lax.broadcasted_iota(jnp.int32, left.shape, 1)
    left_f, right_f = left.astype(F32), right.astype(F32)
    first = jnp.where(lane < HD, left_f, pltpu.roll(right_f, HD, 1))
    second = jnp.where(lane < HD, pltpu.roll(left_f, HD, 1), right_f)
    return first, second


def sort_halo(send_ref, order_ref, keep_ref, last_ref, has_ref, place):
    blocks, groups = last_ref.shape[0], order_ref.shape[0]

    def clear(b, carry):
        has_ref[b] = 0
        return carry

    def count(g, carry):
        has_ref[send_ref[0, g]] += 1
        return carry

    def begin(b, at):
        place[b] = at
        after = at + has_ref[b]
        last_ref[b] = jnp.maximum(after - 1, 0)
        return after

    def put(g, carry):
        b = send_ref[0, g]
        at = place[b]
        order_ref[at] = g
        keep_ref[at] = jnp.where(at > last_ref[b] + 1 - has_ref[b], 1, 0)
        place[b] = at + 1
        return carry

    lax.fori_loop(0, blocks, clear, 0)
    lax.fori_loop(0, groups, count, 0)
    lax.fori_loop(0, blocks, begin, 0)
    lax.fori_loop(0, groups, put, 0)


def attend_kernel(
    send_ref,
    list_ref,
    count_ref,
    qg_ref,
    own_kv,
    halo_kv,
    aq_ref,
    own_ref,
    halo_ref,
    att_t,
    order_ref,
    keep_ref,
    last_ref,
    has_ref,
    kv_ref,
    kv_t,
    acc,
    place,
):
    blocks, rows, _ = qg_ref.shape
    space = kv_ref.shape[0]
    listed = list_ref.shape[1]
    scale = 1.0 / math.sqrt(HD)

    def prepare(part, base):
        def step(i, carry):
            block = part[i]
            kv_ref[base + i] = block
            kv_t[base + i] = block.T
            acc[base + i] = jnp.zeros(acc.shape[1:], F32)
            return carry

        lax.fori_loop(0, part.shape[0], step, 0, unroll=4)

    prepare(own_kv, 0)
    prepare(halo_kv, blocks)
    sort_halo(send_ref, order_ref, keep_ref, last_ref, has_ref, place)

    def one(b, live):
        qg = qg_ref[b]
        lane = lax.broadcasted_iota(jnp.int32, qg.shape, 1)
        full = qg.astype(F32)
        x = jnp.concatenate(
            (
                jnp.where(lane < HD, full * scale, 0.0).astype(BF),
                jnp.where(lane < HD, 0.0, full).astype(BF),
            ),
            axis=0,
        )
        index = [list_ref[b, t] for t in range(live)]
        keys = jnp.concatenate([kv_ref[i] for i in index], axis=0)
        both = lax.dot_general(keys, x, (((1,), (1,)), ((), ())), preferred_element_type=F32)
        scores, dprobs = both[:, :rows], both[:, rows:]
        weights = jnp.exp(scores - jnp.max(scores, axis=0, keepdims=True))
        inverse = 1.0 / jnp.sum(weights, axis=0, keepdims=True)
        probs = weights * inverse
        inner = jnp.sum(probs * dprobs, axis=0, keepdims=True)
        z = jnp.concatenate((probs * (dprobs - inner), probs), axis=1).astype(BF)
        pair = jnp.dot(z, x, preferred_element_type=F32)
        for t, i in enumerate(index):
            acc[i] += pair[t * rows : (t + 1) * rows]
        turned = jnp.concatenate([kv_t[i] for i in index], axis=1)
        out = jnp.dot(turned, z, preferred_element_type=F32)
        attended = out[HD:, rows:]
        att_t[:, pl.ds(pl.multiple_of(b * rows, rows), rows)] = attended.astype(BF)
        aq_ref[b] = jnp.concatenate((out[:HD, :rows] * scale, attended), axis=0).T.astype(BF)

    def step(b, carry):
        count = count_ref[0, b]
        for live in range(1, listed + 1):
            pl.when(count == live)(functools.partial(one, b, live))
        return carry

    lax.fori_loop(0, blocks, step, 0)
    own_ref[...] = acc[:blocks]
    halo_ref[...] = acc[blocks:].astype(BF)


def unpack_kernel(aq_ref, kv_ref, w_ref, out_ref, dq_ref, dk_ref, dv_ref, att):
    for j in range(aq_ref.shape[0] // 2):
        cols = slice(j * LANES, (j + 1) * LANES)
        first, second = weave(aq_ref[2 * j], aq_ref[2 * j + 1])
        dq_ref[:, cols] = first.astype(BF)
        att[:, cols] = second.astype(BF)
        first, second = weave(kv_ref[2 * j], kv_ref[2 * j + 1])
        dk_ref[:, cols] = first.astype(BF)
        dv_ref[:, cols] = second.astype(BF)
    out_ref[...] = jnp.dot(att[...], w_ref[...], preferred_element_type=F32).astype(BF)


def shape(dims, kind=BF):
    return jax.ShapeDtypeStruct(dims, kind)


def call(kernel, in_specs, out_shape, scratch=(), **kw):
    return pl.pallas_call(
        kernel,
        in_specs=in_specs,
        out_specs=jax.tree.map(lambda _: VMEM, out_shape),
        out_shape=out_shape,
        scratch_shapes=list(scratch),
        compiler_params=pltpu.CompilerParams(vmem_limit_bytes=LIMIT),
        **kw,
    )


def attend(send, lists, counts, qg, own_kv, halo_kv):
    blocks, rows, lanes = qg.shape
    groups = halo_kv.shape[0]
    space = blocks + groups
    ints = [shape((n,), jnp.int32) for n in (groups, groups, blocks, blocks)]
    return pl.pallas_call(
        attend_kernel,
        in_specs=[SMEM] * 3 + [VMEM] * 3,
        out_specs=(VMEM,) * 4 + (SMEM,) * 4,
        out_shape=(
            shape((blocks, rows, lanes)),
            shape((blocks, rows, lanes), F32),
            shape((groups, rows, lanes)),
            shape((HD, blocks * rows)),
            *ints,
        ),
        scratch_shapes=[
            pltpu.VMEM((space, rows, lanes), BF),
            pltpu.VMEM((space, lanes, rows), BF),
            pltpu.VMEM((space, rows, lanes), F32),
            pltpu.SMEM((blocks,), jnp.int32),
        ],
        compiler_params=pltpu.CompilerParams(vmem_limit_bytes=LIMIT),
    )(send, lists, counts, qg, own_kv, halo_kv)


def signal(semaphore, seq, grp):
    pl.semaphore_signal(semaphore, inc=1, device_id=(seq, grp), device_id_type=MESH)


def others(count, body):
    def step(k, carry):
        body(k)
        return carry

    lax.fori_loop(1, count, step, 0)


def push(src, dst, send, recv, seq, grp):
    return pltpu.make_async_remote_copy(
        src_ref=src,
        dst_ref=dst,
        send_sem=send,
        recv_sem=recv,
        device_id=(seq, grp),
        device_id_type=MESH,
    )


def bring_kernel(
    send_ref,
    q_ref,
    k_ref,
    v_ref,
    c_ref,
    w_hbm,
    kv_ref,
    halo_ref,
    qg_ref,
    kv_out,
    qg_out,
    halo_out,
    w_ref,
    w_sem,
    kv_send,
    kv_recv,
    qg_send,
    qg_recv,
    halo_send,
    halo_recv,
):
    seq, grp = lax.axis_index("seq"), lax.axis_index("grp")
    n_seq, n_grp = kv_ref.shape[0], halo_ref.shape[0]
    load_w = pltpu.make_async_copy(w_hbm, w_ref, w_sem)
    load_w.start()
    barrier = pltpu.get_barrier_semaphore()
    others(n_seq, lambda k: signal(barrier, lax.rem(seq + k, n_seq), grp))
    others(n_grp, lambda k: signal(barrier, seq, lax.rem(grp + k, n_grp)))

    tiles = [slice(j * LANES, (j + 1) * LANES) for j in range(n_seq // 2)]
    for j, cols in enumerate(tiles):
        first, second = weave(k_ref[:, cols], v_ref[:, cols])
        kv_out[2 * j] = first.astype(BF)
        kv_out[2 * j + 1] = second.astype(BF)
    pl.semaphore_wait(barrier, n_seq + n_grp - 2)

    def kv_copy(k):
        to = lax.rem(seq + k, n_seq)
        return push(kv_out.at[to], kv_ref.at[seq], kv_send.at[k], kv_recv.at[k], to, grp)

    def qg_copy(k):
        to = lax.rem(seq + k, n_seq)
        return push(qg_out.at[to], qg_ref.at[seq], qg_send.at[k], qg_recv.at[k], to, grp)

    def halo_copy(k):
        to = lax.rem(grp + k, n_grp)
        return push(halo_out.at[to], halo_ref.at[grp], halo_send.at[k], halo_recv.at[k], seq, to)

    others(n_seq, lambda k: kv_copy(k).start())
    load_w.wait()
    grad = lax.dot_general(
        c_ref[...], w_ref[...], (((1,), (1,)), ((), ())), preferred_element_type=F32
    ).astype(BF)
    for j, cols in enumerate(tiles):
        first, second = weave(q_ref[:, cols], grad[:, cols])
        qg_out[2 * j] = first.astype(BF)
        qg_out[2 * j + 1] = second.astype(BF)
    others(n_seq, lambda k: qg_copy(k).start())
    kv_ref[seq] = kv_out[seq]
    qg_ref[seq] = qg_out[seq]
    others(n_seq, lambda k: kv_copy(k).wait_recv())

    def forward(k):
        to = lax.rem(grp + k, n_grp)
        halo_out[to] = kv_ref[send_ref[0, to]]
        halo_copy(k).start()

    others(n_grp, forward)
    halo_ref[grp] = kv_ref[send_ref[0, grp]]
    others(n_seq, lambda k: qg_copy(k).wait_recv())
    others(n_grp, lambda k: halo_copy(k).wait_recv())
    others(n_seq, lambda k: kv_copy(k).wait_send())
    others(n_seq, lambda k: qg_copy(k).wait_send())
    others(n_grp, lambda k: halo_copy(k).wait_send())


def bring(send, q, k, v, cot, weight, n_seq, n_grp):
    tile = (q.shape[0], LANES)
    return pl.pallas_call(
        bring_kernel,
        in_specs=[SMEM, VMEM, VMEM, VMEM, VMEM, pl.BlockSpec(memory_space=pl.ANY)],
        out_specs=(VMEM,) * 3,
        out_shape=(shape((n_seq,) + tile), shape((n_grp,) + tile), shape((n_seq,) + tile)),
        scratch_shapes=[
            pltpu.VMEM((n_seq,) + tile, BF),
            pltpu.VMEM((n_seq,) + tile, BF),
            pltpu.VMEM((n_grp,) + tile, BF),
            pltpu.VMEM(weight.shape, BF),
            pltpu.SemaphoreType.DMA,
        ]
        + [pltpu.SemaphoreType.DMA((n,)) for n in (n_seq,) * 4 + (n_grp,) * 2],
        compiler_params=pltpu.CompilerParams(
            vmem_limit_bytes=LIMIT, collective_id=0, has_side_effects=True
        ),
    )(send, q, k, v, cot, weight)


def return_kernel(
    inverse_root,
    order_ref,
    keep_ref,
    last_ref,
    has_ref,
    aq_ref,
    own_ref,
    halo_ref,
    att_ref,
    cot_hbm,
    aq_out,
    kv_out,
    wg_out,
    cot_ref,
    back,
    running,
    dkv,
    term,
    parts,
    share,
    cot_sem,
    aq_send,
    aq_recv,
    kv_send,
    kv_recv,
    halo_send,
    halo_recv,
    part_send,
    part_recv,
    wg_send,
    wg_recv,
):
    seq, grp = lax.axis_index("seq"), lax.axis_index("grp")
    n_seq, n_grp = aq_ref.shape[0], halo_ref.shape[0]
    half = wg_out.shape[0] // 2
    load_cot = pltpu.make_async_copy(cot_hbm, cot_ref, cot_sem)
    load_cot.start()
    barrier = pltpu.get_barrier_semaphore()
    others(n_seq, lambda k: signal(barrier, lax.rem(seq + k, n_seq), grp))
    others(n_grp, lambda k: signal(barrier, seq, lax.rem(grp + k, n_grp)))
    source = grp // 2

    def greet(g, carry):
        @pl.when((source != seq) | (g != grp))
        def _():
            signal(barrier, source, g)

        return carry

    lax.fori_loop(0, n_grp, greet, 0)
    keeps_one = grp // 2 == seq
    pl.semaphore_wait(barrier, n_seq + n_grp - 2 + 2 * n_seq - jnp.where(keeps_one, 1, 0))

    def aq_copy(k):
        to = lax.rem(seq + k, n_seq)
        return push(aq_ref.at[to], aq_out.at[seq], aq_send.at[k], aq_recv.at[k], to, grp)

    def kv_copy(k):
        to = lax.rem(seq + k, n_seq)
        return push(dkv.at[to], kv_out.at[seq], kv_send.at[k], kv_recv.at[k], to, grp)

    def halo_copy(k):
        to = lax.rem(grp + k, n_grp)
        return push(halo_ref.at[to], back.at[grp], halo_send.at[k], halo_recv.at[k], seq, to)

    def corner(piece):
        return (
            pl.ds(pl.multiple_of((piece % 2) * half, half), half),
            pl.ds(pl.multiple_of((piece // 2) * LANES, LANES), LANES),
        )

    def part_copy(row, piece):
        rows, cols = corner(piece)
        return push(
            term.at[row, rows, cols],
            parts.at[grp],
            part_send.at[row, piece],
            part_recv.at[grp],
            piece,
            2 * seq + row,
        )

    def wg_copy(k):
        to = lax.rem(seq + k, n_seq)
        return push(share, wg_out.at[corner(seq)], wg_send.at[k], wg_recv.at[k], to, grp)

    def wg_arrival(k):
        come = lax.rem(seq + n_seq - k, n_seq)
        return push(share, wg_out.at[corner(come)], wg_send.at[k], wg_recv.at[k], come, grp)

    others(n_grp, lambda k: halo_copy(k).start())
    others(n_seq, lambda k: aq_copy(k).start())
    aq_out[seq] = aq_ref[seq]
    back[grp] = halo_ref[grp]

    load_cot.wait()
    total = jnp.dot(att_ref[...], cot_ref[...], preferred_element_type=F32) * inverse_root
    term[0] = total[: 2 * half]
    term[1] = total[2 * half :]

    def elsewhere(row, piece):
        return (piece != seq) | (2 * seq + row != grp)

    def each_part(body):
        for row in range(2):

            def step(piece, carry, row=row):
                pl.when(elsewhere(row, piece))(lambda: body(row, piece))
                return carry

            lax.fori_loop(0, n_seq, step, 0)

    each_part(lambda row, piece: part_copy(row, piece).start())

    @pl.when(keeps_one)
    def _():
        rows, cols = corner(seq)
        parts[grp] = term[grp % 2, rows, cols]

    def part_wait(g, carry):
        @pl.when((source != seq) | (g != grp))
        def _():
            push(
                term.at[0, :half, :LANES],
                parts.at[g],
                part_send.at[0, 0],
                part_recv.at[g],
                source,
                g,
            ).wait_recv()

        return carry

    lax.fori_loop(0, n_grp, part_wait, 0)
    share[...] = jnp.sum(parts[...], axis=0)
    others(n_seq, lambda k: wg_copy(k).start())
    rows, cols = corner(seq)
    wg_out[rows, cols] = share[...]

    others(n_grp, lambda k: halo_copy(k).wait_recv())

    def run(j, total):
        total = jnp.where(keep_ref[j] != 0, total, 0.0) + back[order_ref[j]].astype(F32)
        running[j] = total
        return total

    lax.fori_loop(0, n_grp, run, jnp.zeros(running.shape[1:], F32))

    def settle(b, carry):
        more = jnp.where(has_ref[b] != 0, running[last_ref[b]], 0.0)
        dkv[b] = (own_ref[b] + more).astype(BF)
        return carry

    lax.fori_loop(0, n_seq, settle, 0)
    others(n_seq, lambda k: kv_copy(k).start())
    kv_out[seq] = dkv[seq]

    others(n_seq, lambda k: aq_copy(k).wait_recv())
    others(n_seq, lambda k: wg_arrival(k).wait_recv())
    others(n_seq, lambda k: kv_copy(k).wait_recv())
    others(n_grp, lambda k: halo_copy(k).wait_send())
    others(n_seq, lambda k: aq_copy(k).wait_send())
    each_part(lambda row, piece: part_copy(row, piece).wait_send())
    others(n_seq, lambda k: wg_copy(k).wait_send())
    others(n_seq, lambda k: kv_copy(k).wait_send())


def bring_back(lists, aq, own, halo, att, cot, inverse_root):
    n_seq, n_grp = aq.shape[0], halo.shape[0]
    tile = aq.shape[1:]
    width = cot.shape[1]
    per_group = width // n_grp
    return pl.pallas_call(
        functools.partial(return_kernel, inverse_root),
        in_specs=[SMEM] * 4 + [VMEM] * 4 + [pl.BlockSpec(memory_space=pl.ANY)],
        out_specs=(VMEM,) * 3,
        out_shape=(shape(aq.shape), shape(aq.shape), shape((per_group, width), F32)),
        scratch_shapes=[
            pltpu.VMEM(cot.shape, BF),
            pltpu.VMEM(halo.shape, BF),
            pltpu.VMEM((n_grp,) + tile, F32),
            pltpu.VMEM(aq.shape, BF),
            pltpu.VMEM((2, per_group, width), F32),
            pltpu.VMEM((n_grp, per_group // 2, LANES), F32),
            pltpu.VMEM((per_group // 2, LANES), F32),
            pltpu.SemaphoreType.DMA,
        ]
        + [pltpu.SemaphoreType.DMA((n,)) for n in (n_seq,) * 4 + (n_grp,) * 2]
        + [
            pltpu.SemaphoreType.DMA((2, n_seq)),
            pltpu.SemaphoreType.DMA((n_grp,)),
            pltpu.SemaphoreType.DMA((n_seq,)),
            pltpu.SemaphoreType.DMA((n_seq,)),
        ],
        compiler_params=pltpu.CompilerParams(
            vmem_limit_bytes=LIMIT, collective_id=1, has_side_effects=True
        ),
    )(*lists, aq, own, halo, att, cot)


def per_device(
    queries, key_rows, value_rows, cotangent, out_weight, send_lists, key_blocks, key_counts
):
    n_seq = lax.axis_size("seq")
    n_grp = lax.axis_size("grp")
    rows, width = queries.shape
    send = send_lists[:, :, 0]
    kv, halo, qg = bring(
        send, queries, key_rows, value_rows, cotangent, out_weight, n_seq, n_grp
    )
    cot = lax.all_gather(cotangent, "seq", axis=0, tiled=True)
    aq, own, halo, att, *lists = attend(send, key_blocks[0], key_counts, qg, kv, halo)
    inverse_root = 1.0 / math.sqrt(float(rows * n_seq * n_grp))
    aq, dkv, weight_grad = bring_back(lists, aq, own, halo, att, cot, inverse_root)
    flat = shape((rows, width))
    layer_out, dq, dk, dv = call(
        unpack_kernel, [VMEM] * 3, (flat,) * 4, [pltpu.VMEM((rows, width), BF)]
    )(aq, dkv, out_weight)
    return layer_out, dq, dk, dv, weight_grad


def solution(mesh):
    nodes = P(("seq", "grp"), None)
    by_group = P("grp", None, None)
    return jax.shard_map(
        per_device,
        mesh=mesh,
        in_specs=(nodes, nodes, nodes, nodes, P(), by_group, by_group, P("grp", None)),
        out_specs=(nodes, nodes, nodes, nodes, P("grp", None)),
        check_vma=False,
    )
```

```python
import functools
import math

import jax
import jax.numpy as jnp
from jax import lax
from jax.experimental import pallas as pl
from jax.experimental.pallas import tpu as pltpu
from jax.sharding import PartitionSpec as P

HD = 64
LANES = 128
BF = jnp.bfloat16
F32 = jnp.float32
VMEM = pl.BlockSpec(memory_space=pltpu.VMEM)
SMEM = pl.BlockSpec(memory_space=pltpu.SMEM)
ANY = pl.BlockSpec(memory_space=pl.ANY)
LIMIT = 60 * 1024 * 1024
CHUNKS = 2
MESH = pl.DeviceIdType.MESH


def weave(left, right):
    lane = lax.broadcasted_iota(jnp.int32, left.shape, 1)
    left_f, right_f = left.astype(F32), right.astype(F32)
    first = jnp.where(lane < HD, left_f, pltpu.roll(right_f, HD, 1))
    second = jnp.where(lane < HD, pltpu.roll(left_f, HD, 1), right_f)
    return first, second


def shape(dims, kind=BF):
    return jax.ShapeDtypeStruct(dims, kind)


def signal(semaphore, seq, grp):
    pl.semaphore_signal(semaphore, inc=1, device_id=(seq, grp), device_id_type=MESH)


def others(count, body):
    def step(k, carry):
        body(k)
        return carry

    lax.fori_loop(1, count, step, 0)


def each(count, body, unroll=1):
    def step(i, carry):
        body(i)
        return carry

    lax.fori_loop(0, count, step, 0, unroll=unroll)


def push(src, dst, send, recv, seq, grp):
    return pltpu.make_async_remote_copy(
        src_ref=src,
        dst_ref=dst,
        send_sem=send,
        recv_sem=recv,
        device_id=(seq, grp),
        device_id_type=MESH,
    )


def local(src, dst, semaphore):
    return pltpu.make_async_copy(src, dst, semaphore)


def rows_of(ref, block, chunk):
    rows = ref.shape[1] // CHUNKS
    return ref.at[block, pl.ds(chunk * rows, rows)]


def place_order(place):
    row = lax.broadcasted_iota(jnp.int32, place.shape, 0).astype(F32)
    col = lax.broadcasted_iota(jnp.int32, place.shape, 1).astype(F32)
    other = place.T
    earlier = (other < place) | ((other == place) & (col < row))
    rank = jnp.sum(jnp.where(earlier, 1.0, 0.0), axis=1, keepdims=True)
    there = rank == col

    def down(mask, value):
        return jnp.sum(jnp.where(mask, value, 0.0), axis=0, keepdims=True)

    order = down(there, row)
    sorted_place = down(there, place)
    again = (sorted_place == pltpu.roll(sorted_place, 1, 1)) & (col[:1] > 0.0)
    last = jnp.maximum(down(place <= col, 1.0) - 1.0, 0.0)
    return jnp.concatenate(
        (order, jnp.where(again, 1.0, 0.0), last, down(place == col, 1.0)), axis=0
    ).astype(jnp.int32)


def plan_kernel(send_ref, list_ref, plan_ref, place):
    listed, blocks = list_ref.shape[1:]
    groups = send_ref.shape[2]

    def put(i, value):
        place[pl.ds(i, 1), :] = jnp.full((1, place.shape[1]), value, jnp.int32)

    def pairs(b):
        for t in range(listed):
            put(b * listed + t, list_ref[0, t, b])

    each(blocks, pairs)
    for_pairs = place_order(place[...].astype(F32))
    place[...] = jnp.full(place.shape, place.shape[1], jnp.int32)
    each(groups, lambda g: put(g, send_ref[0, 0, g]))
    plan_ref[...] = jnp.concatenate((for_pairs, place_order(place[...].astype(F32))), axis=0)


def make_plan(send, lists):
    items = lists.shape[1] * lists.shape[2]
    return pl.pallas_call(
        plan_kernel,
        in_specs=[SMEM] * 2,
        out_specs=VMEM,
        out_shape=shape((8, items), jnp.int32),
        scratch_shapes=[pltpu.VMEM((items, items), jnp.int32)],
    )(send, lists)


def split_pair(pair):
    lane = lax.broadcasted_iota(jnp.int32, pair.shape, 1)
    full = pair.astype(F32)
    scale = 1.0 / math.sqrt(HD)
    return jnp.concatenate(
        (
            jnp.where(lane < HD, full * scale, 0.0).astype(BF),
            jnp.where(lane < HD, 0.0, full).astype(BF),
        ),
        axis=0,
    )


def attend_blocks(blocks, list_ref, count_ref, x_ref, kv_ref, kv_t, aq_ref, att_t, terms):
    listed = list_ref.shape[1]
    rows = kv_ref.shape[1]
    scale = 1.0 / math.sqrt(HD)
    span = range(listed)
    index = [[list_ref[0, t, b] for t in span] for b in blocks]
    xs = [x_ref[b] for b in blocks]
    both = [
        lax.dot_general(
            jnp.concatenate([kv_ref[i] for i in at], axis=0),
            x,
            (((1,), (1,)), ((), ())),
            preferred_element_type=F32,
        )
        for at, x in zip(index, xs)
    ]
    zs = []
    for b, pair in zip(blocks, both):
        bias = [jnp.where(count_ref[0, b] > t, 0.0, -jnp.inf).astype(F32) for t in span]
        scores = [pair[t * rows : (t + 1) * rows, :rows] + bias[t] for t in span]
        dprobs = [pair[t * rows : (t + 1) * rows, rows:] for t in span]
        top = functools.reduce(jnp.maximum, scores)
        top = jnp.max(top, axis=0, keepdims=True)
        weights = [jnp.exp(s - top) for s in scores]
        inverse = 1.0 / jnp.sum(sum(weights), axis=0, keepdims=True)
        inner = sum(w * d for w, d in zip(weights, dprobs))
        inner = jnp.sum(inner, axis=0, keepdims=True) * inverse
        z = []
        for w, d in zip(weights, dprobs):
            probs = w * inverse
            z.append(jnp.concatenate((probs * (d - inner), probs), axis=1).astype(BF))
        zs.append(z)
    for b, z, x in zip(blocks, zs, xs):
        pair = jnp.dot(jnp.concatenate(z, axis=0), x, preferred_element_type=F32)
        for t in span:
            terms[b * listed + t] = pair[t * rows : (t + 1) * rows]
    for b, z, at in zip(blocks, zs, index):
        turned = jnp.concatenate([kv_t[i] for i in at], axis=1)
        out = jnp.dot(turned, jnp.concatenate(z, axis=0), preferred_element_type=F32)
        attended = out[HD:, rows:]
        att_t[b] = attended.astype(BF)
        aq_ref[b] = jnp.concatenate((out[:HD, :rows] * scale, attended), axis=0).T.astype(BF)


def sums_by_place(plan_ref, at, source, running):
    def run(j, total):
        total = jnp.where(plan_ref[at + 1, j] != 0, total, 0.0)
        total = total + source[plan_ref[at, j]].astype(F32)
        running[j] = total
        return total

    lax.fori_loop(0, running.shape[0], run, jnp.zeros(running.shape[1:], F32), unroll=4)


def sum_of(place, plan_ref, at, running):
    return jnp.where(plan_ref[at + 3, place] != 0, running[plan_ref[at + 2, place]], 0.0)


OFFSETS = (0, -1, 1, -2, 2, -3, 3, 4)
SIDE = 4


def layer_kernel(
    inverse_root,
    send_ref,
    list_ref,
    count_ref,
    plan_ref,
    q_hbm,
    k_hbm,
    v_hbm,
    c_hbm,
    w_hbm,
    out_hbm,
    dq_hbm,
    kv_back,
    wg_out,
    q_ref,
    k_ref,
    v_ref,
    c_ref,
    w_ref,
    kv_out,
    kv_in,
    qg_out,
    qg_in,
    halo_out,
    kv_ref,
    kv_t,
    x_ref,
    terms,
    running,
    aq_out,
    aq_in,
    att_t,
    att_n,
    own_grad,
    halo_grad,
    back,
    back_sum,
    dkv,
    cot_ref,
    total,
    term,
    parts,
    share,
    load_sem,
    local_sem,
    ring_send,
    ring_recv,
    core_send,
    core_recv,
    kv_send,
    kv_recv,
    qg_send,
    qg_recv,
    halo_send,
    halo_recv,
    aq_send,
    aq_recv,
    hg_send,
    hg_recv,
    dkv_send,
    dkv_recv,
    part_send,
    part_recv,
    wg_send,
    wg_recv,
):
    seq, grp = lax.axis_index("seq"), lax.axis_index("grp")
    n_seq, n_grp = qg_in.shape[0], halo_grad.shape[0]
    size = kv_in[0].shape[1]
    half = wg_out.shape[0] // 2
    middle = cot_ref.shape[2] // 2
    right, left = lax.rem(seq + 2, n_seq), lax.rem(seq + n_seq - 2, n_seq)
    core = lax.rem(seq, 2)
    sibling = seq + 1 - 2 * core
    source = grp // 2
    keeps_one = source == seq
    tiles = [slice(j * LANES, (j + 1) * LANES) for j in range(n_seq // 2)]

    pairs = ((k_hbm, k_ref), (v_hbm, v_ref), (c_hbm, c_ref), (w_hbm, w_ref), (q_hbm, q_ref))
    loads = [local(src, dst, load_sem.at[i]) for i, (src, dst) in enumerate(pairs)]
    for load in loads:
        load.start()
    barrier = pltpu.get_barrier_semaphore()
    others(n_seq, lambda k: signal(barrier, lax.rem(seq + k, n_seq), grp))
    others(n_grp, lambda k: signal(barrier, seq, lax.rem(grp + k, n_grp)))

    def from_source(g, body):
        pl.when((source != seq) | (g != grp))(body)

    each(n_grp, lambda g: from_source(g, lambda: signal(barrier, source, g)))

    def kv_copy(c, k):
        to = lax.rem(seq + k, n_seq)
        return push(
            rows_of(kv_out, to, c), kv_in[c].at[seq], kv_send.at[c, k], kv_recv.at[c, k], to, grp
        )

    def qg_copy(k):
        to = lax.rem(seq + k, n_seq)
        return push(qg_out.at[to], qg_in.at[seq], qg_send.at[k], qg_recv.at[k], to, grp)

    def halo_copy(c, k):
        to = lax.rem(grp + k, n_grp)
        return push(
            halo_out.at[c, to],
            rows_of(kv_ref, n_seq + grp, c),
            halo_send.at[c, k],
            halo_recv.at[c, k],
            seq,
            to,
        )

    def halo_arrival(c, k):
        come = lax.rem(grp + n_grp - k, n_grp)
        return push(
            halo_out.at[c, come],
            rows_of(kv_ref, n_seq + come, c),
            halo_send.at[c, k],
            halo_recv.at[c, k],
            seq,
            come,
        )

    def aq_copy(b):
        return push(aq_out.at[b], aq_in.at[seq], aq_send.at[b], aq_recv.at[seq], b, grp)

    def aq_arrival(b):
        return push(aq_out.at[b], aq_in.at[b], aq_send.at[b], aq_recv.at[b], b, grp)

    def hg_copy(c, k):
        to = lax.rem(grp + k, n_grp)
        return push(
            rows_of(halo_grad, to, c), back[c].at[grp], hg_send.at[c, k], hg_recv.at[c, k], seq, to
        )

    def dkv_copy(c, k):
        to = lax.rem(seq + k, n_seq)
        return push(
            dkv.at[c, to], rows_of(kv_back, seq, c), dkv_send.at[c, k], dkv_recv.at[c, k], to, grp
        )

    def ring_copy(i, src, dst):
        to = right if i % 2 == 0 else left
        return push(src, dst, ring_send.at[i], ring_recv.at[i], to, grp)

    def core_copy(slot):
        return push(
            cot_ref.at[slot, 0],
            cot_ref.at[slot, 1],
            core_send.at[slot],
            core_recv.at[slot],
            sibling,
            grp,
        )

    def corner(piece):
        return (
            pl.ds(pl.multiple_of((piece % 2) * half, half), half),
            pl.ds(pl.multiple_of((piece // 2) * LANES, LANES), LANES),
        )

    def part_copy(row, piece):
        rows, cols = corner(piece)
        return push(
            term.at[row, rows, cols],
            parts.at[grp],
            part_send.at[row, piece],
            part_recv.at[grp],
            piece,
            2 * seq + row,
        )

    def part_arrival(g):
        return push(
            term.at[0, :half, :LANES],
            parts.at[g],
            part_send.at[0, 0],
            part_recv.at[g],
            source,
            g,
        )

    def each_part(body):
        for row in range(2):

            def step(piece, row=row):
                elsewhere = (piece != seq) | (2 * seq + row != grp)
                pl.when(elsewhere)(lambda: body(row, piece))

            each(n_seq, step)

    def wg_copy(k):
        to = lax.rem(seq + k, n_seq)
        return push(share, wg_out.at[corner(seq)], wg_send.at[k], wg_recv.at[k], to, grp)

    def wg_arrival(k):
        come = lax.rem(seq + n_seq - k, n_seq)
        return push(share, wg_out.at[corner(come)], wg_send.at[k], wg_recv.at[k], come, grp)

    loads[0].wait()
    loads[1].wait()
    for j, cols in enumerate(tiles):
        first, second = weave(k_ref[:, cols], v_ref[:, cols])
        kv_out[2 * j] = first.astype(BF)
        kv_out[2 * j + 1] = second.astype(BF)
    pl.semaphore_wait(barrier, n_seq + n_grp - 2 + 2 * n_seq - jnp.where(keeps_one, 1, 0))
    others(n_seq, lambda k: kv_copy(0, k).start())
    for load in loads[2:]:
        load.wait()
    grad = lax.dot_general(
        c_ref[...], w_ref[...], (((1,), (1,)), ((), ())), preferred_element_type=F32
    ).astype(BF)
    for j, cols in enumerate(tiles):
        first, second = weave(q_ref[:, cols], grad[:, cols])
        qg_out[2 * j] = first.astype(BF)
        qg_out[2 * j + 1] = second.astype(BF)
    cot_ref[0, 0] = c_ref[...]
    qg_in[seq] = qg_out[seq]
    others(n_seq, lambda k: kv_copy(0, k).wait_send())
    others(n_seq, lambda k: kv_copy(1, k).start())

    def pass_on(c):
        mine = kv_in[c]
        mine[seq] = kv_out[seq, c * size : (c + 1) * size]
        others(n_seq, lambda k: kv_copy(c, k).wait_recv())

        def forward(k):
            to = lax.rem(grp + k, n_grp)
            halo_out[c, to] = mine[send_ref[0, 0, to]]
            halo_copy(c, k).start()

        others(n_grp, forward)
        kv_ref[n_seq + grp, c * size : (c + 1) * size] = mine[send_ref[0, 0, grp]]
        kv_ref[:n_seq, c * size : (c + 1) * size] = mine[...]

    pass_on(0)
    others(n_seq, lambda k: kv_copy(1, k).wait_send())
    others(n_seq, lambda k: qg_copy(k).start())
    pass_on(1)

    def turn(i):
        kv_t[i] = kv_ref[i].T

    each(n_seq, turn, 4)
    turn(n_seq + grp)
    others(n_seq, lambda k: qg_copy(k).wait_send())
    rings = [ring_copy(0, cot_ref.at[0, 0], cot_ref.at[1, 0])]
    rings.append(ring_copy(1, cot_ref.at[0, 0], cot_ref.at[2, 0]))
    for copy in rings:
        copy.start()
    core_copy(0).start()
    others(n_seq, lambda k: qg_copy(k).wait_recv())

    def prepare(b):
        x_ref[b] = split_pair(qg_in[b])

    each(n_seq, prepare, 2)

    def take(k):
        for c in range(CHUNKS):
            halo_arrival(c, k).wait_recv()
        turn(n_seq + lax.rem(grp + n_grp - k, n_grp))

    others(n_grp, take)

    for i in range(2, 6):
        rings.append(ring_copy(i, cot_ref.at[i - 1, 0], cot_ref.at[i + 1, 0]))

    def step(i):
        blocks = [i * SIDE + j for j in range(SIDE)]
        attend_blocks(
            blocks, list_ref, count_ref, x_ref, kv_ref, kv_t, aq_out, att_t, terms
        )
        for b in blocks:
            pl.when(b != seq)(aq_copy(b).start)

        @pl.when(i == 0)
        def _():
            for way in range(2):
                rings[way].wait_recv()
                rings[2 + way].start()
                core_copy(1 + way).start()

    each(n_seq // SIDE, step)
    aq_in[seq] = aq_out[seq]

    sums_by_place(plan_ref, 0, terms, running)

    def give(k):
        to = lax.rem(grp + k, n_grp)
        halo_grad[to] = sum_of(n_seq + to, plan_ref, 0, running).astype(BF)
        hg_copy(0, k).start()

    others(n_grp, give)
    mine = sum_of(n_seq + grp, plan_ref, 0, running).astype(BF)
    for c in range(CHUNKS):
        back[c][grp] = mine[c * size : (c + 1) * size]
    for way in range(2):
        rings[2 + way].wait_recv()
        rings[4 + way].start()
        core_copy(3 + way).start()

    def keep(b):
        own_grad[b] = sum_of(b, plan_ref, 0, running)

    each(n_seq, keep, 4)

    def block_of(offset, of_core):
        return lax.rem(seq - core + 2 * offset + n_seq, n_seq) + of_core

    def add(slot):
        core_copy(slot).wait_recv()
        att = jnp.concatenate(
            (att_t[block_of(OFFSETS[slot], core)], att_t[block_of(OFFSETS[slot], 1 - core)]),
            axis=1,
        )
        cot = cot_ref[slot].reshape(att.shape[1], cot_ref.shape[3])
        part = jnp.dot(att, cot, preferred_element_type=F32) * inverse_root
        total[...] = part if slot == 0 else total[...] + part

    for slot in range(3):
        add(slot)
    others(n_grp, lambda k: hg_copy(0, k).wait_send())
    others(n_grp, lambda k: hg_copy(1, k).start())
    for slot in range(3, 5):
        add(slot)
    for way in range(2):
        rings[4 + way].wait_recv()
        where = pl.ds(way * middle, middle)
        rings.append(ring_copy(6 + way, cot_ref.at[5 + way, 0, where], cot_ref.at[7, 0, where]))
        rings[-1].start()
        core_copy(5 + way).start()

    others(n_seq, lambda k: aq_arrival(lax.rem(seq + k, n_seq)).wait_recv())
    for j, cols in enumerate(tiles):
        first, second = weave(aq_in[2 * j], aq_in[2 * j + 1])
        q_ref[:, cols] = first.astype(BF)
        att_n[:, cols] = second.astype(BF)
    k_ref[...] = jnp.dot(att_n[...], w_ref[...], preferred_element_type=F32).astype(BF)
    stores = [local(q_ref, dq_hbm, local_sem.at[0]), local(k_ref, out_hbm, local_sem.at[1])]
    for store in stores:
        store.start()
    for slot in range(5, 7):
        add(slot)

    def settle(c):
        others(n_grp, lambda k: hg_copy(c, k).wait_recv())
        sums_by_place(plan_ref, 4, back[c], back_sum)

        def finish(b):
            more = sum_of(b, plan_ref, 4, back_sum)
            dkv[c, b] = (own_grad[b, c * size : (c + 1) * size] + more).astype(BF)

        each(n_seq, finish, 4)
        others(n_seq, lambda k: dkv_copy(c, k).start())
        stores.append(local(dkv.at[c, seq], rows_of(kv_back, seq, c), local_sem.at[2 + c]))
        stores[-1].start()

    settle(0)
    for way in range(2):
        rings[6 + way].wait_recv()
    core_copy(7).start()
    add(7)
    for row in range(2):
        term[row] = total[2 * half * row : 2 * half * (row + 1)].astype(BF)
    each_part(lambda row, piece: part_copy(row, piece).start())

    @pl.when(keeps_one)
    def _():
        rows, cols = corner(seq)
        parts[grp] = term[lax.rem(grp, 2), rows, cols]

    settle(1)
    each(n_grp, lambda g: from_source(g, part_arrival(g).wait_recv))
    share[...] = jnp.sum(parts[...].astype(F32), axis=0)
    others(n_seq, lambda k: wg_copy(k).start())
    rows, cols = corner(seq)
    wg_out[rows, cols] = share[...]

    for copy in rings:
        copy.wait_send()
    for slot in range(len(OFFSETS)):
        core_copy(slot).wait_send()
    for c in range(CHUNKS):
        others(n_grp, lambda k, c=c: halo_copy(c, k).wait_send())
    others(n_seq, lambda k: aq_copy(lax.rem(seq + k, n_seq)).wait_send())
    others(n_grp, lambda k: hg_copy(1, k).wait_send())
    each_part(lambda row, piece: part_copy(row, piece).wait_send())
    others(n_seq, lambda k: wg_copy(k).wait_send())
    others(n_seq, lambda k: wg_arrival(k).wait_recv())
    for c in range(CHUNKS):
        others(n_seq, lambda k, c=c: dkv_copy(c, k).wait_recv())
        others(n_seq, lambda k, c=c: dkv_copy(c, k).wait_send())
    for store in stores:
        store.wait()


def layer(send, lists, counts, plan, q, k, v, cot, weight, n_seq, n_grp):
    rows, width = q.shape
    tile, part = (rows, LANES), (rows // CHUNKS, LANES)
    per_group = width // n_grp
    space = n_seq + n_grp
    items = lists.shape[1] * lists.shape[2]
    dma = pltpu.SemaphoreType.DMA
    inverse_root = 1.0 / math.sqrt(float(rows * n_seq * n_grp))
    return pl.pallas_call(
        functools.partial(layer_kernel, inverse_root),
        in_specs=[SMEM] * 4 + [ANY] * 5,
        out_specs=(ANY, ANY, ANY, VMEM),
        out_shape=(
            shape(q.shape),
            shape(q.shape),
            shape((n_seq,) + tile),
            shape((per_group, width), F32),
        ),
        scratch_shapes=[pltpu.VMEM(q.shape, BF)] * 4
        + [
            pltpu.VMEM(weight.shape, BF),
            pltpu.VMEM((n_seq,) + tile, BF),
            [pltpu.VMEM((n_seq,) + part, BF)] * CHUNKS,
            pltpu.VMEM((n_seq,) + tile, BF),
            pltpu.VMEM((n_seq,) + tile, BF),
            pltpu.VMEM((CHUNKS, n_grp) + part, BF),
            pltpu.VMEM((space,) + tile, BF),
            pltpu.VMEM((space, LANES, rows), BF),
            pltpu.VMEM((n_seq, 2 * rows, LANES), BF),
            pltpu.VMEM((items,) + tile, F32),
            pltpu.VMEM((items,) + tile, F32),
            pltpu.VMEM((n_seq,) + tile, BF),
            pltpu.VMEM((n_seq,) + tile, BF),
            pltpu.VMEM((n_seq, HD, rows), BF),
            pltpu.VMEM(q.shape, BF),
            pltpu.VMEM((n_seq,) + tile, F32),
            pltpu.VMEM((n_grp,) + tile, BF),
            [pltpu.VMEM((n_grp,) + part, BF)] * CHUNKS,
            pltpu.VMEM((n_grp,) + part, F32),
            pltpu.VMEM((CHUNKS, n_seq) + part, BF),
            pltpu.VMEM((len(OFFSETS), 2) + cot.shape, BF),
            pltpu.VMEM((HD, width), F32),
            pltpu.VMEM((2, per_group, width), BF),
            pltpu.VMEM((n_grp, per_group // 2, LANES), BF),
            pltpu.VMEM((per_group // 2, LANES), F32),
            dma((5,)),
            dma((2 + CHUNKS,)),
            dma((8,)),
            dma((8,)),
            dma((len(OFFSETS),)),
            dma((len(OFFSETS),)),
            dma((CHUNKS, n_seq)),
            dma((CHUNKS, n_seq)),
            dma((n_seq,)),
            dma((n_seq,)),
            dma((CHUNKS, n_grp)),
            dma((CHUNKS, n_grp)),
            dma((n_seq,)),
            dma((n_seq,)),
            dma((CHUNKS, n_grp)),
            dma((CHUNKS, n_grp)),
            dma((CHUNKS, n_seq)),
            dma((CHUNKS, n_seq)),
            dma((2, n_seq)),
            dma((n_grp,)),
            dma((n_seq,)),
            dma((n_seq,)),
        ],
        compiler_params=pltpu.CompilerParams(
            vmem_limit_bytes=LIMIT, collective_id=0, has_side_effects=True
        ),
    )(send, lists, counts, plan, q, k, v, cot, weight)


def finish_kernel(out_in, dq_in, kv_ref, wg_in, out_ref, dq_ref, dk_ref, dv_ref, wg_ref):
    out_ref[...] = out_in[...]
    dq_ref[...] = dq_in[...]
    wg_ref[...] = wg_in[...]
    for j in range(kv_ref.shape[0] // 2):
        cols = slice(j * LANES, (j + 1) * LANES)
        first, second = weave(kv_ref[2 * j], kv_ref[2 * j + 1])
        dk_ref[:, cols] = first.astype(BF)
        dv_ref[:, cols] = second.astype(BF)


def per_device(
    queries, key_rows, value_rows, cotangent, out_weight, send_lists, key_blocks, key_counts
):
    send = send_lists.transpose(0, 2, 1)
    lists = key_blocks.transpose(0, 2, 1)
    out, dq, dkv, weight_grad = layer(
        send,
        lists,
        key_counts,
        make_plan(send, lists),
        queries,
        key_rows,
        value_rows,
        cotangent,
        out_weight,
        lax.axis_size("seq"),
        lax.axis_size("grp"),
    )
    flat = shape(queries.shape)
    return pl.pallas_call(
        finish_kernel,
        in_specs=[VMEM] * 4,
        out_specs=(VMEM,) * 5,
        out_shape=(flat,) * 4 + (shape(weight_grad.shape, F32),),
        compiler_params=pltpu.CompilerParams(vmem_limit_bytes=LIMIT),
    )(out, dq, dkv, weight_grad)


def solution(mesh):
    nodes = P(("seq", "grp"), None)
    by_group = P("grp", None, None)
    return jax.shard_map(
        per_device,
        mesh=mesh,
        in_specs=(nodes, nodes, nodes, nodes, P(), by_group, by_group, P("grp", None)),
        out_specs=(nodes, nodes, nodes, nodes, P("grp", None)),
        check_vma=False,
    )
```

```python
import functools
import math

import jax
import jax.numpy as jnp
from jax import lax
from jax.experimental import pallas as pl
from jax.experimental.pallas import tpu as pltpu
from jax.sharding import PartitionSpec as P

HD = 64
LANES = 128
BF = jnp.bfloat16
F32 = jnp.float32
VMEM = pl.BlockSpec(memory_space=pltpu.VMEM)
SMEM = pl.BlockSpec(memory_space=pltpu.SMEM)
ANY = pl.BlockSpec(memory_space=pl.ANY)
LIMIT = 60 * 1024 * 1024
THERE = (64, 64)
BACK = (64, 64)
MESH = pl.DeviceIdType.MESH


def weave(left, right):
    lane = lax.broadcasted_iota(jnp.int32, left.shape, 1)
    left_f, right_f = left.astype(F32), right.astype(F32)
    first = jnp.where(lane < HD, left_f, pltpu.roll(right_f, HD, 1))
    second = jnp.where(lane < HD, pltpu.roll(left_f, HD, 1), right_f)
    return first, second


def shape(dims, kind=BF):
    return jax.ShapeDtypeStruct(dims, kind)


def signal(semaphore, seq, grp):
    pl.semaphore_signal(semaphore, inc=1, device_id=(seq, grp), device_id_type=MESH)


def others(count, body):
    def step(k, carry):
        body(k)
        return carry

    lax.fori_loop(1, count, step, 0)


def each(count, body, unroll=1):
    def step(i, carry):
        body(i)
        return carry

    lax.fori_loop(0, count, step, 0, unroll=unroll)


def push(src, dst, send, recv, seq, grp):
    return pltpu.make_async_remote_copy(
        src_ref=src,
        dst_ref=dst,
        send_sem=send,
        recv_sem=recv,
        device_id=(seq, grp),
        device_id_type=MESH,
    )


def local(src, dst, semaphore):
    return pltpu.make_async_copy(src, dst, semaphore)


def span_of(sizes, c):
    return slice(sum(sizes[:c]), sum(sizes[: c + 1]))


def rows_of(ref, block, sizes, c):
    return ref.at[block, pl.ds(sum(sizes[:c]), sizes[c])]


def place_order(place):
    row = lax.broadcasted_iota(jnp.int32, place.shape, 0).astype(F32)
    col = lax.broadcasted_iota(jnp.int32, place.shape, 1).astype(F32)
    other = place.T
    earlier = (other < place) | ((other == place) & (col < row))
    rank = jnp.sum(jnp.where(earlier, 1.0, 0.0), axis=1, keepdims=True)
    there = rank == col

    def down(mask, value):
        return jnp.sum(jnp.where(mask, value, 0.0), axis=0, keepdims=True)

    order = down(there, row)
    sorted_place = down(there, place)
    again = (sorted_place == pltpu.roll(sorted_place, 1, 1)) & (col[:1] > 0.0)
    last = jnp.maximum(down(place <= col, 1.0) - 1.0, 0.0)
    return jnp.concatenate(
        (order, jnp.where(again, 1.0, 0.0), last, down(place == col, 1.0)), axis=0
    ).astype(jnp.int32)


def plan_kernel(send_ref, list_ref, plan_ref, place):
    listed, blocks = list_ref.shape[1:]
    groups = send_ref.shape[2]

    def put(i, value):
        place[pl.ds(i, 1), :] = jnp.full((1, place.shape[1]), value, jnp.int32)

    def pairs(b):
        for t in range(listed):
            put(b * listed + t, list_ref[0, t, b])

    each(blocks, pairs)
    for_pairs = place_order(place[...].astype(F32))
    place[...] = jnp.full(place.shape, place.shape[1], jnp.int32)
    each(groups, lambda g: put(g, send_ref[0, 0, g]))
    plan_ref[...] = jnp.concatenate((for_pairs, place_order(place[...].astype(F32))), axis=0)


def make_plan(send, lists):
    items = lists.shape[1] * lists.shape[2]
    return pl.pallas_call(
        plan_kernel,
        in_specs=[SMEM] * 2,
        out_specs=VMEM,
        out_shape=shape((8, items), jnp.int32),
        scratch_shapes=[pltpu.VMEM((items, items), jnp.int32)],
    )(send, lists)


def split_pair(pair):
    lane = lax.broadcasted_iota(jnp.int32, pair.shape, 1)
    full = pair.astype(F32)
    scale = 1.0 / math.sqrt(HD)
    return jnp.concatenate(
        (
            jnp.where(lane < HD, full * scale, 0.0).astype(BF),
            jnp.where(lane < HD, 0.0, full).astype(BF),
        ),
        axis=0,
    )


def attend_blocks(blocks, list_ref, count_ref, x_ref, kv_ref, kv_t, aq_ref, att_t, terms):
    listed = list_ref.shape[1]
    rows = kv_ref.shape[1]
    scale = 1.0 / math.sqrt(HD)
    span = range(listed)
    index = [[list_ref[0, t, b] for t in span] for b in blocks]
    xs = [x_ref[b] for b in blocks]
    both = [
        lax.dot_general(
            jnp.concatenate([kv_ref[i] for i in at], axis=0),
            x,
            (((1,), (1,)), ((), ())),
            preferred_element_type=F32,
        )
        for at, x in zip(index, xs)
    ]
    zs = []
    for b, pair in zip(blocks, both):
        bias = [jnp.where(count_ref[0, b] > t, 0.0, -jnp.inf).astype(F32) for t in span]
        scores = [pair[t * rows : (t + 1) * rows, :rows] + bias[t] for t in span]
        dprobs = [pair[t * rows : (t + 1) * rows, rows:] for t in span]
        top = functools.reduce(jnp.maximum, scores)
        top = jnp.max(top, axis=0, keepdims=True)
        weights = [jnp.exp(s - top) for s in scores]
        inverse = 1.0 / jnp.sum(sum(weights), axis=0, keepdims=True)
        inner = sum(w * d for w, d in zip(weights, dprobs))
        inner = jnp.sum(inner, axis=0, keepdims=True) * inverse
        z = []
        for w, d in zip(weights, dprobs):
            probs = w * inverse
            z.append(jnp.concatenate((probs * (d - inner), probs), axis=1).astype(BF))
        zs.append(z)
    for b, z, x in zip(blocks, zs, xs):
        pair = jnp.dot(jnp.concatenate(z, axis=0), x, preferred_element_type=F32)
        for t in span:
            terms[b * listed + t] = pair[t * rows : (t + 1) * rows]
    for b, z, at in zip(blocks, zs, index):
        turned = jnp.concatenate([kv_t[i] for i in at], axis=1)
        out = jnp.dot(turned, jnp.concatenate(z, axis=0), preferred_element_type=F32)
        attended = out[HD:, rows:]
        att_t[b] = attended.astype(BF)
        aq_ref[b] = jnp.concatenate((out[:HD, :rows] * scale, attended), axis=0).T.astype(BF)


def sums_by_place(plan_ref, at, source, running):
    def run(j, total):
        total = jnp.where(plan_ref[at + 1, j] != 0, total, 0.0)
        total = total + source[plan_ref[at, j]].astype(F32)
        running[j] = total
        return total

    lax.fori_loop(0, running.shape[0], run, jnp.zeros(running.shape[1:], F32), unroll=4)


def sum_of(place, plan_ref, at, running):
    return jnp.where(plan_ref[at + 3, place] != 0, running[plan_ref[at + 2, place]], 0.0)


OFFSETS = (0, -1, 1, -2, 2, -3, 3, 4)
SIDE = 4


def layer_kernel(
    inverse_root,
    send_ref,
    list_ref,
    count_ref,
    plan_ref,
    q_hbm,
    k_hbm,
    v_hbm,
    c_hbm,
    w_hbm,
    out_hbm,
    dq_hbm,
    kv_back,
    wg_out,
    q_ref,
    k_ref,
    v_ref,
    c_ref,
    w_ref,
    kv_out,
    kv_in,
    qg_out,
    qg_in,
    halo_out,
    kv_ref,
    kv_t,
    x_ref,
    terms,
    running,
    aq_out,
    aq_in,
    att_t,
    att_n,
    own_grad,
    halo_grad,
    back,
    back_sum,
    dkv,
    cot_ref,
    total,
    term,
    parts,
    share,
    wg_in,
    load_sem,
    local_sem,
    ring_send,
    ring_recv,
    core_send,
    core_recv,
    kv_send,
    kv_recv,
    qg_send,
    qg_recv,
    halo_send,
    halo_recv,
    aq_send,
    aq_recv,
    hg_send,
    hg_recv,
    dkv_send,
    dkv_recv,
    part_send,
    part_recv,
    wg_send,
    wg_recv,
):
    seq, grp = lax.axis_index("seq"), lax.axis_index("grp")
    n_seq, n_grp = qg_in.shape[0], halo_grad.shape[0]
    half = wg_out.shape[0] // 2
    middle = cot_ref.shape[2] // 2
    right, left = lax.rem(seq + 2, n_seq), lax.rem(seq + n_seq - 2, n_seq)
    core = lax.rem(seq, 2)
    sibling = seq + 1 - 2 * core
    next_grp = lax.rem(grp + 1, n_grp)
    source = grp // 2
    keeps_one = source == seq
    tiles = [slice(j * LANES, (j + 1) * LANES) for j in range(n_seq // 2)]

    pairs = ((k_hbm, k_ref), (v_hbm, v_ref), (c_hbm, c_ref), (w_hbm, w_ref), (q_hbm, q_ref))
    loads = [local(src, dst, load_sem.at[i]) for i, (src, dst) in enumerate(pairs)]
    for load in loads:
        load.start()
    barrier = pltpu.get_barrier_semaphore()
    others(n_seq, lambda k: signal(barrier, lax.rem(seq + k, n_seq), grp))
    others(n_grp, lambda k: signal(barrier, seq, lax.rem(grp + k, n_grp)))

    def greet(g):
        pl.when((source != seq) | (g != grp))(lambda: signal(barrier, source, g))

    each(n_grp, greet)

    most, rest = pl.ds(0, n_seq - 1), pl.ds(0, n_grp - 1)

    def kv_copy(c, to, src=None, dst=None):
        src = rows_of(kv_out, to, THERE, c) if src is None else src
        dst = kv_in[c].at[seq] if dst is None else dst
        return push(src, dst, kv_send.at[c], kv_recv.at[c], to, grp)

    def all_kv(c):
        src = rows_of(kv_out, most, THERE, c)
        return kv_copy(c, sibling, src, kv_in[c].at[most])

    def qg_copy(to, src=None, dst=None):
        src = qg_out.at[to] if src is None else src
        dst = qg_in.at[seq] if dst is None else dst
        return push(src, dst, qg_send, qg_recv, to, grp)

    def all_qg():
        return qg_copy(sibling, qg_out.at[most], qg_in.at[most])

    def halo_copy(c, to, src=None, dst=None):
        src = halo_out[c].at[to] if src is None else src
        dst = rows_of(kv_ref, n_seq + grp, THERE, c) if dst is None else dst
        return push(src, dst, halo_send.at[c], halo_recv.at[c], seq, to)

    def all_halo(c):
        dst = rows_of(kv_ref, pl.ds(n_seq, n_grp - 1), THERE, c)
        return halo_copy(c, next_grp, halo_out[c].at[rest], dst)

    def aq_copy(to, src=None, dst=None):
        src = aq_out.at[to] if src is None else src
        dst = aq_in.at[seq] if dst is None else dst
        return push(src, dst, aq_send, aq_recv, to, grp)

    def all_aq():
        return aq_copy(sibling, aq_out.at[most], aq_in.at[most])

    def hg_copy(c, to, src=None, dst=None):
        src = rows_of(halo_grad, to, BACK, c) if src is None else src
        dst = back[c].at[grp] if dst is None else dst
        return push(src, dst, hg_send.at[c], hg_recv.at[c], seq, to)

    def all_hg(c):
        return hg_copy(c, next_grp, rows_of(halo_grad, rest, BACK, c), back[c].at[rest])

    def dkv_copy(c, to, src=None, dst=None):
        src = dkv[c].at[to] if src is None else src
        dst = rows_of(kv_back, seq, BACK, c) if dst is None else dst
        return push(src, dst, dkv_send.at[c], dkv_recv.at[c], to, grp)

    def all_dkv(c):
        return dkv_copy(c, sibling, dkv[c].at[most], rows_of(kv_back, most, BACK, c))

    def to_seq(body):
        others(n_seq, lambda k: body(lax.rem(seq + k, n_seq)))

    def to_grp(body):
        others(n_grp, lambda k: body(lax.rem(grp + k, n_grp)))

    def ring_copy(i, src, dst):
        to = right if i % 2 == 0 else left
        return push(src, dst, ring_send.at[i], ring_recv.at[i], to, grp)

    def core_copy(slot):
        return push(
            cot_ref.at[slot, 0],
            cot_ref.at[slot, 1],
            core_send.at[slot],
            core_recv.at[slot],
            sibling,
            grp,
        )

    def corner(piece):
        return (
            pl.ds(pl.multiple_of((piece % 2) * half, half), half),
            pl.ds(pl.multiple_of((piece // 2) * LANES, LANES), LANES),
        )

    def part_copy(row, piece):
        rows, cols = corner(piece)
        return push(
            term.at[row, rows, cols], parts.at[grp], part_send, part_recv, piece, 2 * seq + row
        )

    def all_parts(body):
        for mine in (0, 1):
            every = parts.at[pl.ds(0, n_grp - mine)]
            copy = push(every, every, part_send, part_recv, sibling, grp)
            pl.when(keeps_one if mine else jnp.logical_not(keeps_one))(functools.partial(body, copy))

    def each_part(body):
        for row in range(2):

            def step(piece, row=row):
                elsewhere = (piece != seq) | (2 * seq + row != grp)
                pl.when(elsewhere)(lambda: body(row, piece))

            each(n_seq, step)

    def wg_copy(to):
        return push(share, wg_in.at[seq], wg_send, wg_recv, to, grp)

    def all_wg():
        return push(wg_in.at[most], wg_in.at[most], wg_send, wg_recv, sibling, grp)

    loads[0].wait()
    loads[1].wait()
    for j, cols in enumerate(tiles):
        first, second = weave(k_ref[:, cols], v_ref[:, cols])
        kv_out[2 * j] = first.astype(BF)
        kv_out[2 * j + 1] = second.astype(BF)
    pl.semaphore_wait(barrier, n_seq + n_grp - 2 + 2 * n_seq - jnp.where(keeps_one, 1, 0))
    to_seq(lambda to: kv_copy(0, to).start())
    for load in loads[2:]:
        load.wait()
    grad = lax.dot_general(
        c_ref[...], w_ref[...], (((1,), (1,)), ((), ())), preferred_element_type=F32
    ).astype(BF)
    for j, cols in enumerate(tiles):
        first, second = weave(q_ref[:, cols], grad[:, cols])
        qg_out[2 * j] = first.astype(BF)
        qg_out[2 * j + 1] = second.astype(BF)
    cot_ref[0, 0] = c_ref[...]
    qg_in[seq] = qg_out[seq]
    def pass_on(c):
        mine, span = kv_in[c], span_of(THERE, c)
        mine[seq] = kv_out[seq, span]
        all_kv(c).wait_recv()

        def forward(to):
            halo_out[c][to] = mine[send_ref[0, 0, to]]
            halo_copy(c, to).start()

        to_grp(forward)
        kv_ref[n_seq + grp, span] = mine[send_ref[0, 0, grp]]
        kv_ref[:n_seq, span] = mine[...]

    for c in range(1, len(THERE)):
        all_kv(c - 1).wait_send()
        to_seq(lambda to, c=c: kv_copy(c, to).start())
        pass_on(c - 1)
    all_kv(len(THERE) - 1).wait_send()
    to_seq(lambda to: qg_copy(to).start())
    pass_on(len(THERE) - 1)

    def turn(i):
        kv_t[i] = kv_ref[i].T

    each(n_seq, turn, 4)
    all_qg().wait_send()
    rings = [ring_copy(0, cot_ref.at[0, 0], cot_ref.at[1, 0])]
    rings.append(ring_copy(1, cot_ref.at[0, 0], cot_ref.at[2, 0]))
    for copy in rings:
        copy.start()
    core_copy(0).start()
    all_qg().wait_recv()

    def prepare(b):
        x_ref[b] = split_pair(qg_in[b])

    each(n_seq, prepare, 2)
    for c in range(len(THERE)):
        all_halo(c).wait_recv()
    each(n_grp, lambda g: turn(n_seq + g), 4)
    for i in range(2, 6):
        rings.append(ring_copy(i, cot_ref.at[i - 1, 0], cot_ref.at[i + 1, 0]))

    def ring_step(first):
        for way in range(2):
            rings[first + way].wait_recv()
            rings[first + 2 + way].start()
            core_copy(first + 1 + way).start()

    def step(i):
        blocks = [i * SIDE + j for j in range(SIDE)]
        attend_blocks(
            blocks, list_ref, count_ref, x_ref, kv_ref, kv_t, aq_out, att_t, terms
        )
        for b in blocks:
            pl.when(b != seq)(aq_copy(b).start)
        pl.when(i == 0)(lambda: ring_step(0))

    each(n_seq // SIDE, step)
    aq_in[seq] = aq_out[seq]

    sums_by_place(plan_ref, 0, terms, running)

    def give(to):
        halo_grad[to] = sum_of(n_seq + to, plan_ref, 0, running).astype(BF)
        hg_copy(0, to).start()

    to_grp(give)
    mine = sum_of(n_seq + grp, plan_ref, 0, running).astype(BF)
    for c in range(len(BACK)):
        back[c][grp] = mine[span_of(BACK, c)]
    ring_step(2)

    def keep(b):
        own_grad[b] = sum_of(b, plan_ref, 0, running)

    each(n_seq, keep, 4)

    def block_of(offset, of_core):
        return lax.rem(seq - core + 2 * offset + n_seq, n_seq) + of_core

    def add(slot):
        core_copy(slot).wait_recv()
        att = jnp.concatenate(
            (att_t[block_of(OFFSETS[slot], core)], att_t[block_of(OFFSETS[slot], 1 - core)]),
            axis=1,
        )
        cot = cot_ref[slot].reshape(att.shape[1], cot_ref.shape[3])
        part = jnp.dot(att, cot, preferred_element_type=F32) * inverse_root
        total[...] = part if slot == 0 else total[...] + part

    for slot in range(5):
        add(slot)
    for c in range(1, len(BACK)):
        all_hg(c - 1).wait_send()
        to_grp(lambda to, c=c: hg_copy(c, to).start())
    for way in range(2):
        rings[4 + way].wait_recv()
        where = pl.ds(way * middle, middle)
        rings.append(ring_copy(6 + way, cot_ref.at[5 + way, 0, where], cot_ref.at[7, 0, where]))
        rings[-1].start()
        core_copy(5 + way).start()

    all_aq().wait_recv()
    for j, cols in enumerate(tiles):
        first, second = weave(aq_in[2 * j], aq_in[2 * j + 1])
        q_ref[:, cols] = first.astype(BF)
        att_n[:, cols] = second.astype(BF)
    k_ref[...] = jnp.dot(att_n[...], w_ref[...], preferred_element_type=F32).astype(BF)
    stores = [local(q_ref, dq_hbm, local_sem.at[0]), local(k_ref, out_hbm, local_sem.at[1])]
    for store in stores:
        store.start()
    for slot in range(5, 7):
        add(slot)

    def settle(c):
        span = span_of(BACK, c)
        all_hg(c).wait_recv()
        sums_by_place(plan_ref, 4, back[c], back_sum[c])

        def finish(b):
            more = sum_of(b, plan_ref, 4, back_sum[c])
            dkv[c][b] = (own_grad[b, span] + more).astype(BF)

        each(n_seq, finish, 4)
        to_seq(lambda to: dkv_copy(c, to).start())
        stores.append(local(dkv[c].at[seq], rows_of(kv_back, seq, BACK, c), local_sem.at[2 + c]))
        stores[-1].start()

    for c in range(len(BACK) - 1):
        settle(c)
    for way in range(2):
        rings[6 + way].wait_recv()
    core_copy(7).start()
    add(7)
    for row in range(2):
        term[row] = total[2 * half * row : 2 * half * (row + 1)].astype(BF)
    each_part(lambda row, piece: part_copy(row, piece).start())

    @pl.when(keeps_one)
    def _():
        rows, cols = corner(seq)
        parts[grp] = term[lax.rem(grp, 2), rows, cols]

    settle(len(BACK) - 1)
    all_parts(lambda copy: copy.wait_recv())
    share[...] = jnp.sum(parts[...].astype(F32), axis=0)
    to_seq(lambda to: wg_copy(to).start())
    wg_in[seq] = share[...]

    for copy in rings:
        copy.wait_send()
    for slot in range(len(OFFSETS)):
        core_copy(slot).wait_send()
    for c in range(len(THERE)):
        all_halo(c).wait_send()
    all_aq().wait_send()
    all_hg(len(BACK) - 1).wait_send()
    all_parts(lambda copy: copy.wait_send())
    all_wg().wait_send()
    all_wg().wait_recv()
    for piece in range(n_seq):
        rows, cols = corner(piece)
        wg_out[rows, cols] = wg_in[piece]
    for c in range(len(BACK)):
        all_dkv(c).wait_send()
    for c in range(len(BACK)):
        all_dkv(c).wait_recv()
    for store in stores:
        store.wait()


def layer(send, lists, counts, plan, q, k, v, cot, weight, n_seq, n_grp):
    rows, width = q.shape
    tile = (rows, LANES)
    per_group = width // n_grp
    space = n_seq + n_grp
    items = lists.shape[1] * lists.shape[2]
    dma = pltpu.SemaphoreType.DMA
    inverse_root = 1.0 / math.sqrt(float(rows * n_seq * n_grp))
    return pl.pallas_call(
        functools.partial(layer_kernel, inverse_root),
        in_specs=[SMEM] * 4 + [ANY] * 5,
        out_specs=(ANY, ANY, ANY, VMEM),
        out_shape=(
            shape(q.shape),
            shape(q.shape),
            shape((n_seq,) + tile),
            shape((per_group, width), F32),
        ),
        scratch_shapes=[pltpu.VMEM(q.shape, BF)] * 4
        + [
            pltpu.VMEM(weight.shape, BF),
            pltpu.VMEM((n_seq,) + tile, BF),
            [pltpu.VMEM((n_seq, size, LANES), BF) for size in THERE],
            pltpu.VMEM((n_seq,) + tile, BF),
            pltpu.VMEM((n_seq,) + tile, BF),
            [pltpu.VMEM((n_grp, size, LANES), BF) for size in THERE],
            pltpu.VMEM((space,) + tile, BF),
            pltpu.VMEM((space, LANES, rows), BF),
            pltpu.VMEM((n_seq, 2 * rows, LANES), BF),
            pltpu.VMEM((items,) + tile, F32),
            pltpu.VMEM((items,) + tile, F32),
            pltpu.VMEM((n_seq,) + tile, BF),
            pltpu.VMEM((n_seq,) + tile, BF),
            pltpu.VMEM((n_seq, HD, rows), BF),
            pltpu.VMEM(q.shape, BF),
            pltpu.VMEM((n_seq,) + tile, F32),
            pltpu.VMEM((n_grp,) + tile, BF),
            [pltpu.VMEM((n_grp, size, LANES), BF) for size in BACK],
            [pltpu.VMEM((n_grp, size, LANES), F32) for size in BACK],
            [pltpu.VMEM((n_seq, size, LANES), BF) for size in BACK],
            pltpu.VMEM((len(OFFSETS), 2) + cot.shape, BF),
            pltpu.VMEM((HD, width), F32),
            pltpu.VMEM((2, per_group, width), BF),
            pltpu.VMEM((n_grp, per_group // 2, LANES), BF),
            pltpu.VMEM((per_group // 2, LANES), F32),
            pltpu.VMEM((n_seq, per_group // 2, LANES), F32),
            dma((5,)),
            dma((2 + len(BACK),)),
            dma((8,)),
            dma((8,)),
            dma((len(OFFSETS),)),
            dma((len(OFFSETS),)),
            dma((len(THERE),)),
            dma((len(THERE),)),
            dma,
            dma,
            dma((len(THERE),)),
            dma((len(THERE),)),
            dma,
            dma,
            dma((len(BACK),)),
            dma((len(BACK),)),
            dma((len(BACK),)),
            dma((len(BACK),)),
            dma,
            dma,
            dma,
            dma,
        ],
        compiler_params=pltpu.CompilerParams(
            vmem_limit_bytes=LIMIT, collective_id=0, has_side_effects=True
        ),
    )(send, lists, counts, plan, q, k, v, cot, weight)


def finish_kernel(out_in, dq_in, kv_ref, wg_in, out_ref, dq_ref, dk_ref, dv_ref, wg_ref):
    out_ref[...] = out_in[...]
    dq_ref[...] = dq_in[...]
    wg_ref[...] = wg_in[...]
    for j in range(kv_ref.shape[0] // 2):
        cols = slice(j * LANES, (j + 1) * LANES)
        first, second = weave(kv_ref[2 * j], kv_ref[2 * j + 1])
        dk_ref[:, cols] = first.astype(BF)
        dv_ref[:, cols] = second.astype(BF)


def per_device(
    queries, key_rows, value_rows, cotangent, out_weight, send_lists, key_blocks, key_counts
):
    send = send_lists.transpose(0, 2, 1)
    lists = key_blocks.transpose(0, 2, 1)
    out, dq, dkv, weight_grad = layer(
        send,
        lists,
        key_counts,
        make_plan(send, lists),
        queries,
        key_rows,
        value_rows,
        cotangent,
        out_weight,
        lax.axis_size("seq"),
        lax.axis_size("grp"),
    )
    flat = shape(queries.shape)
    return pl.pallas_call(
        finish_kernel,
        in_specs=[VMEM] * 4,
        out_specs=(VMEM,) * 5,
        out_shape=(flat,) * 4 + (shape(weight_grad.shape, F32),),
        compiler_params=pltpu.CompilerParams(vmem_limit_bytes=LIMIT),
    )(out, dq, dkv, weight_grad)


def solution(mesh):
    nodes = P(("seq", "grp"), None)
    by_group = P("grp", None, None)
    return jax.shard_map(
        per_device,
        mesh=mesh,
        in_specs=(nodes, nodes, nodes, nodes, P(), by_group, by_group, P("grp", None)),
        out_specs=(nodes, nodes, nodes, nodes, P("grp", None)),
        check_vma=False,
    )
```

```python
import functools
import math

import jax
import jax.numpy as jnp
from jax import lax
from jax.experimental import pallas as pl
from jax.experimental.pallas import tpu as pltpu
from jax.sharding import PartitionSpec as P

HD = 64
LANES = 128
BF = jnp.bfloat16
F32 = jnp.float32
VMEM = pl.BlockSpec(memory_space=pltpu.VMEM)
SMEM = pl.BlockSpec(memory_space=pltpu.SMEM)
ANY = pl.BlockSpec(memory_space=pl.ANY)
LIMIT = 60 * 1024 * 1024
THERE = (64, 64)
BACK = (64, 64)
MESH = pl.DeviceIdType.MESH


def weave(left, right):
    lane = lax.broadcasted_iota(jnp.int32, left.shape, 1)
    left_f, right_f = left.astype(F32), right.astype(F32)
    first = jnp.where(lane < HD, left_f, pltpu.roll(right_f, HD, 1))
    second = jnp.where(lane < HD, pltpu.roll(left_f, HD, 1), right_f)
    return first, second


def shape(dims, kind=BF):
    return jax.ShapeDtypeStruct(dims, kind)


def signal(semaphore, seq, grp):
    pl.semaphore_signal(semaphore, inc=1, device_id=(seq, grp), device_id_type=MESH)


def others(count, body):
    def step(k, carry):
        body(k)
        return carry

    lax.fori_loop(1, count, step, 0)


def each(count, body, unroll=1):
    def step(i, carry):
        body(i)
        return carry

    lax.fori_loop(0, count, step, 0, unroll=unroll)


def push(src, dst, send, recv, seq, grp):
    return pltpu.make_async_remote_copy(
        src_ref=src,
        dst_ref=dst,
        send_sem=send,
        recv_sem=recv,
        device_id=(seq, grp),
        device_id_type=MESH,
    )


def local(src, dst, semaphore):
    return pltpu.make_async_copy(src, dst, semaphore)


def span_of(sizes, c):
    return slice(sum(sizes[:c]), sum(sizes[: c + 1]))


def rows_of(ref, block, sizes, c):
    return ref.at[block, pl.ds(sum(sizes[:c]), sizes[c])]


def place_order(place):
    row = lax.broadcasted_iota(jnp.int32, place.shape, 0)
    col = lax.broadcasted_iota(jnp.int32, place.shape, 1)
    other = place.T
    earlier = (other < place) | ((other == place) & (col < row))
    rank = jnp.sum(jnp.where(earlier, 1, 0), axis=1, keepdims=True)
    there = rank == col

    def down(mask, value):
        return jnp.sum(jnp.where(mask, value, 0), axis=0, keepdims=True)

    order = down(there, row)
    sorted_place = down(there, place)
    again = (sorted_place == pltpu.roll(sorted_place, 1, 1)) & (col[:1] > 0)
    last = jnp.maximum(down(place <= col, 1) - 1, 0)
    return jnp.concatenate((order, jnp.where(again, 1, 0), last, down(place == col, 1)), axis=0)


def make_plan(send_ref, list_ref, place, plan):
    listed, blocks = list_ref.shape[1:]
    groups = send_ref.shape[2]

    def put(i, value):
        place[pl.ds(i, 1), :] = jnp.full((1, place.shape[1]), value, jnp.int32)

    def pairs(b):
        for t in range(listed):
            put(b * listed + t, list_ref[0, t, b])

    each(blocks, pairs)
    for_pairs = place_order(place[...])
    place[...] = jnp.full(place.shape, place.shape[1], jnp.int32)
    each(groups, lambda g: put(g, send_ref[0, 0, g]))
    plan[...] = jnp.concatenate((for_pairs, place_order(place[...])), axis=0)


def split_pair(pair):
    lane = lax.broadcasted_iota(jnp.int32, pair.shape, 1)
    full = pair.astype(F32)
    scale = 1.0 / math.sqrt(HD)
    return jnp.concatenate(
        (
            jnp.where(lane < HD, full * scale, 0.0).astype(BF),
            jnp.where(lane < HD, 0.0, full).astype(BF),
        ),
        axis=0,
    )


def attend_blocks(blocks, list_ref, count_ref, x_ref, kv_ref, kv_t, aq_ref, att_t, terms):
    listed = list_ref.shape[1]
    rows = kv_ref.shape[1]
    scale = 1.0 / math.sqrt(HD)
    span = range(listed)
    index = [[list_ref[0, t, b] for t in span] for b in blocks]
    xs = [x_ref[b] for b in blocks]
    both = [
        lax.dot_general(
            jnp.concatenate([kv_ref[i] for i in at], axis=0),
            x,
            (((1,), (1,)), ((), ())),
            preferred_element_type=F32,
        )
        for at, x in zip(index, xs)
    ]
    zs = []
    for b, pair in zip(blocks, both):
        bias = [jnp.where(count_ref[0, b] > t, 0.0, -jnp.inf).astype(F32) for t in span]
        scores = [pair[t * rows : (t + 1) * rows, :rows] + bias[t] for t in span]
        dprobs = [pair[t * rows : (t + 1) * rows, rows:] for t in span]
        top = functools.reduce(jnp.maximum, scores)
        top = jnp.max(top, axis=0, keepdims=True)
        weights = [jnp.exp(s - top) for s in scores]
        inverse = 1.0 / jnp.sum(sum(weights), axis=0, keepdims=True)
        inner = sum(w * d for w, d in zip(weights, dprobs))
        inner = jnp.sum(inner, axis=0, keepdims=True) * inverse
        z = []
        for w, d in zip(weights, dprobs):
            probs = w * inverse
            z.append(jnp.concatenate((probs * (d - inner), probs), axis=1).astype(BF))
        zs.append(z)
    for b, z, x in zip(blocks, zs, xs):
        pair = jnp.dot(jnp.concatenate(z, axis=0), x, preferred_element_type=F32)
        for t in span:
            terms[b * listed + t] = pair[t * rows : (t + 1) * rows]
    for b, z, at in zip(blocks, zs, index):
        turned = jnp.concatenate([kv_t[i] for i in at], axis=1)
        out = jnp.dot(turned, jnp.concatenate(z, axis=0), preferred_element_type=F32)
        attended = out[HD:, rows:]
        att_t[b] = attended.astype(BF)
        aq_ref[b] = jnp.concatenate((out[:HD, :rows] * scale, attended), axis=0).T.astype(BF)


def sums_by_place(plan_ref, at, source, running, span=slice(None)):
    def run(j, total):
        total = jnp.where(plan_ref[at + 1, j] != 0, total, 0.0)
        total = total + source[plan_ref[at, j], span].astype(F32)
        running[j, span] = total
        return total

    rows = len(range(*span.indices(running.shape[1])))
    zero = jnp.zeros((rows, running.shape[2]), F32)
    lax.fori_loop(0, running.shape[0], run, zero, unroll=4)


def sum_of(place, plan_ref, at, running, span=slice(None)):
    return jnp.where(plan_ref[at + 3, place] != 0, running[plan_ref[at + 2, place], span], 0.0)


OFFSETS = (0, -1, 1, -2, 2, -3, 3, 4)
SIDE = 4


def layer_kernel(
    inverse_root,
    send_ref,
    list_ref,
    count_ref,
    q_hbm,
    k_hbm,
    v_hbm,
    c_hbm,
    w_hbm,
    out_hbm,
    dq_hbm,
    kv_back,
    wg_out,
    q_ref,
    k_ref,
    v_ref,
    c_ref,
    w_ref,
    kv_out,
    kv_in,
    qg_out,
    qg_in,
    halo_out,
    kv_ref,
    kv_t,
    x_ref,
    terms,
    running,
    aq_out,
    aq_in,
    att_t,
    att_n,
    own_grad,
    halo_grad,
    back,
    back_sum,
    dkv,
    cot_ref,
    total,
    term,
    parts,
    share,
    wg_in,
    place,
    plan,
    plan_ref,
    load_sem,
    local_sem,
    ring_send,
    ring_recv,
    core_send,
    core_recv,
    kv_send,
    kv_recv,
    qg_send,
    qg_recv,
    halo_send,
    halo_recv,
    aq_send,
    aq_recv,
    hg_send,
    hg_recv,
    dkv_send,
    dkv_recv,
    part_send,
    part_recv,
    wg_send,
    wg_recv,
):
    seq, grp = lax.axis_index("seq"), lax.axis_index("grp")
    n_seq, n_grp = qg_in.shape[0], halo_grad.shape[0]
    half = wg_out.shape[0] // 2
    middle = cot_ref.shape[2] // 2
    right, left = lax.rem(seq + 2, n_seq), lax.rem(seq + n_seq - 2, n_seq)
    core = lax.rem(seq, 2)
    sibling = seq + 1 - 2 * core
    next_grp = lax.rem(grp + 1, n_grp)
    source = grp // 2
    keeps_one = source == seq
    tiles = [slice(j * LANES, (j + 1) * LANES) for j in range(n_seq // 2)]

    pairs = ((k_hbm, k_ref), (v_hbm, v_ref), (c_hbm, c_ref), (w_hbm, w_ref), (q_hbm, q_ref))
    loads = [local(src, dst, load_sem.at[i]) for i, (src, dst) in enumerate(pairs)]
    for load in loads:
        load.start()
    barrier = pltpu.get_barrier_semaphore()
    others(n_seq, lambda k: signal(barrier, lax.rem(seq + k, n_seq), grp))
    others(n_grp, lambda k: signal(barrier, seq, lax.rem(grp + k, n_grp)))

    def greet(g):
        pl.when((source != seq) | (g != grp))(lambda: signal(barrier, source, g))

    each(n_grp, greet)

    most, rest = pl.ds(0, n_seq - 1), pl.ds(0, n_grp - 1)

    def kv_copy(c, to, src=None, dst=None):
        src = rows_of(kv_out, to, THERE, c) if src is None else src
        dst = kv_in[c].at[seq] if dst is None else dst
        return push(src, dst, kv_send.at[c], kv_recv.at[c], to, grp)

    def all_kv(c):
        src = rows_of(kv_out, most, THERE, c)
        return kv_copy(c, sibling, src, kv_in[c].at[most])

    def qg_copy(to, src=None, dst=None):
        src = qg_out.at[to] if src is None else src
        dst = qg_in.at[seq] if dst is None else dst
        return push(src, dst, qg_send, qg_recv, to, grp)

    def all_qg():
        return qg_copy(sibling, qg_out.at[most], qg_in.at[most])

    def halo_copy(c, to, src=None, dst=None):
        src = halo_out[c].at[to] if src is None else src
        dst = rows_of(kv_ref, n_seq + grp, THERE, c) if dst is None else dst
        return push(src, dst, halo_send.at[c], halo_recv.at[c], seq, to)

    def all_halo(c):
        dst = rows_of(kv_ref, pl.ds(n_seq, n_grp - 1), THERE, c)
        return halo_copy(c, next_grp, halo_out[c].at[rest], dst)

    def aq_copy(to, src=None, dst=None):
        src = aq_out.at[to] if src is None else src
        dst = aq_in.at[seq] if dst is None else dst
        return push(src, dst, aq_send, aq_recv, to, grp)

    def all_aq():
        return aq_copy(sibling, aq_out.at[most], aq_in.at[most])

    def hg_copy(c, to, src=None, dst=None):
        src = rows_of(halo_grad, to, BACK, c) if src is None else src
        dst = back[c].at[grp] if dst is None else dst
        return push(src, dst, hg_send.at[c], hg_recv.at[c], seq, to)

    def all_hg(c):
        return hg_copy(c, next_grp, rows_of(halo_grad, rest, BACK, c), back[c].at[rest])

    def dkv_copy(c, to, src=None, dst=None):
        src = dkv[c].at[to] if src is None else src
        dst = rows_of(kv_back, seq, BACK, c) if dst is None else dst
        return push(src, dst, dkv_send.at[c], dkv_recv.at[c], to, grp)

    def all_dkv(c):
        return dkv_copy(c, sibling, dkv[c].at[most], rows_of(kv_back, most, BACK, c))

    def to_seq(body):
        others(n_seq, lambda k: body(lax.rem(seq + k, n_seq)))

    def to_grp(body):
        others(n_grp, lambda k: body(lax.rem(grp + k, n_grp)))

    def ring_copy(i, src, dst):
        to = right if i % 2 == 0 else left
        return push(src, dst, ring_send.at[i], ring_recv.at[i], to, grp)

    def core_copy(slot):
        return push(
            cot_ref.at[slot, 0],
            cot_ref.at[slot, 1],
            core_send.at[slot],
            core_recv.at[slot],
            sibling,
            grp,
        )

    def corner(piece):
        return (
            pl.ds(pl.multiple_of((piece % 2) * half, half), half),
            pl.ds(pl.multiple_of((piece // 2) * LANES, LANES), LANES),
        )

    def part_copy(row, piece):
        rows, cols = corner(piece)
        return push(
            term.at[row, rows, cols], parts.at[grp], part_send, part_recv, piece, 2 * seq + row
        )

    def all_parts(body):
        for mine in (0, 1):
            every = parts.at[pl.ds(0, n_grp - mine)]
            copy = push(every, every, part_send, part_recv, sibling, grp)
            pl.when(keeps_one if mine else jnp.logical_not(keeps_one))(functools.partial(body, copy))

    def each_part(body):
        for row in range(2):

            def step(piece, row=row):
                elsewhere = (piece != seq) | (2 * seq + row != grp)
                pl.when(elsewhere)(lambda: body(row, piece))

            each(n_seq, step)

    def wg_copy(to):
        return push(share, wg_in.at[seq], wg_send, wg_recv, to, grp)

    def all_wg():
        return push(wg_in.at[most], wg_in.at[most], wg_send, wg_recv, sibling, grp)

    loads[0].wait()
    loads[1].wait()
    for j, cols in enumerate(tiles):
        first, second = weave(k_ref[:, cols], v_ref[:, cols])
        kv_out[2 * j] = first.astype(BF)
        kv_out[2 * j + 1] = second.astype(BF)
    pl.semaphore_wait(barrier, n_seq + n_grp - 2 + 2 * n_seq - jnp.where(keeps_one, 1, 0))
    to_seq(lambda to: kv_copy(0, to).start())
    for load in loads[2:]:
        load.wait()
    grad = lax.dot_general(
        c_ref[...], w_ref[...], (((1,), (1,)), ((), ())), preferred_element_type=F32
    ).astype(BF)
    for j, cols in enumerate(tiles):
        first, second = weave(q_ref[:, cols], grad[:, cols])
        qg_out[2 * j] = first.astype(BF)
        qg_out[2 * j + 1] = second.astype(BF)
    cot_ref[0, 0] = c_ref[...]
    qg_in[seq] = qg_out[seq]
    def pass_on(c):
        mine, span = kv_in[c], span_of(THERE, c)
        mine[seq] = kv_out[seq, span]
        all_kv(c).wait_recv()

        def forward(to):
            halo_out[c][to] = mine[send_ref[0, 0, to]]
            halo_copy(c, to).start()

        to_grp(forward)
        kv_ref[n_seq + grp, span] = mine[send_ref[0, 0, grp]]
        kv_ref[:n_seq, span] = mine[...]

    for c in range(1, len(THERE)):
        all_kv(c - 1).wait_send()
        to_seq(lambda to, c=c: kv_copy(c, to).start())
        pass_on(c - 1)
    all_kv(len(THERE) - 1).wait_send()
    to_seq(lambda to: qg_copy(to).start())
    pass_on(len(THERE) - 1)

    def turn(i, span=slice(None)):
        kv_t[i, :, span] = kv_ref[i, span].T

    each(n_seq, turn, 4)
    make_plan(send_ref, list_ref, place, plan)
    plan_load = local(plan, plan_ref, load_sem.at[5])
    plan_load.start()
    all_qg().wait_send()
    rings = [ring_copy(0, cot_ref.at[0, 0], cot_ref.at[1, 0])]
    rings.append(ring_copy(1, cot_ref.at[0, 0], cot_ref.at[2, 0]))
    for copy in rings:
        copy.start()
    core_copy(0).start()
    all_qg().wait_recv()

    def prepare(b):
        x_ref[b] = split_pair(qg_in[b])

    each(n_seq, prepare, 2)
    for c in range(len(THERE)):
        all_halo(c).wait_recv()
        each(n_grp, lambda g, c=c: turn(n_seq + g, span_of(THERE, c)), 4)
    for i in range(2, 6):
        rings.append(ring_copy(i, cot_ref.at[i - 1, 0], cot_ref.at[i + 1, 0]))

    def ring_step(first):
        for way in range(2):
            rings[first + way].wait_recv()
            rings[first + 2 + way].start()
            core_copy(first + 1 + way).start()

    plan_load.wait()

    def step(i):
        blocks = [i * SIDE + j for j in range(SIDE)]
        attend_blocks(
            blocks, list_ref, count_ref, x_ref, kv_ref, kv_t, aq_out, att_t, terms
        )
        pl.when(i == 0)(lambda: ring_step(0))

    each(n_seq // SIDE, step)
    aq_in[seq] = aq_out[seq]

    def sum_up(c):
        sums_by_place(plan_ref, 0, terms, running, span_of(BACK, c))

    def give(c, to):
        span = span_of(BACK, c)
        halo_grad[to, span] = sum_of(n_seq + to, plan_ref, 0, running, span).astype(BF)
        hg_copy(c, to).start()

    sum_up(0)
    to_grp(functools.partial(give, 0))
    to_seq(lambda to: aq_copy(to).start())
    ring_step(2)
    for c in range(1, len(BACK)):
        sum_up(c)
    mine = sum_of(n_seq + grp, plan_ref, 0, running).astype(BF)
    for c in range(len(BACK)):
        back[c][grp] = mine[span_of(BACK, c)]

    def keep(b):
        own_grad[b] = sum_of(b, plan_ref, 0, running)

    each(n_seq, keep, 4)

    def block_of(offset, of_core):
        return lax.rem(seq - core + 2 * offset + n_seq, n_seq) + of_core

    def add(slot):
        core_copy(slot).wait_recv()
        att = jnp.concatenate(
            (att_t[block_of(OFFSETS[slot], core)], att_t[block_of(OFFSETS[slot], 1 - core)]),
            axis=1,
        )
        cot = cot_ref[slot].reshape(att.shape[1], cot_ref.shape[3])
        part = jnp.dot(att, cot, preferred_element_type=F32) * inverse_root
        total[...] = part if slot == 0 else total[...] + part

    for slot in range(5):
        add(slot)
    for c in range(1, len(BACK)):
        all_hg(c - 1).wait_send()
        to_grp(functools.partial(give, c))
    for way in range(2):
        rings[4 + way].wait_recv()
        where = pl.ds(way * middle, middle)
        rings.append(ring_copy(6 + way, cot_ref.at[5 + way, 0, where], cot_ref.at[7, 0, where]))
        rings[-1].start()
        core_copy(5 + way).start()

    stores = []

    def settle(c):
        span = span_of(BACK, c)
        all_hg(c).wait_recv()
        sums_by_place(plan_ref, 4, back[c], back_sum[c])

        def finish(b):
            more = sum_of(b, plan_ref, 4, back_sum[c])
            dkv[c][b] = (own_grad[b, span] + more).astype(BF)

        each(n_seq, finish, 4)
        to_seq(lambda to: dkv_copy(c, to).start())
        stores.append(local(dkv[c].at[seq], rows_of(kv_back, seq, BACK, c), local_sem.at[2 + c]))
        stores[-1].start()

    for c in range(len(BACK) - 1):
        settle(c)

    all_aq().wait_recv()
    for j, cols in enumerate(tiles):
        first, second = weave(aq_in[2 * j], aq_in[2 * j + 1])
        q_ref[:, cols] = first.astype(BF)
        att_n[:, cols] = second.astype(BF)
    k_ref[...] = jnp.dot(att_n[...], w_ref[...], preferred_element_type=F32).astype(BF)
    for store in (local(q_ref, dq_hbm, local_sem.at[0]), local(k_ref, out_hbm, local_sem.at[1])):
        store.start()
        stores.append(store)
    for slot in range(5, 7):
        add(slot)

    for way in range(2):
        rings[6 + way].wait_recv()
    core_copy(7).start()
    add(7)
    for row in range(2):
        term[row] = total[2 * half * row : 2 * half * (row + 1)].astype(BF)
    each_part(lambda row, piece: part_copy(row, piece).start())

    @pl.when(keeps_one)
    def _():
        rows, cols = corner(seq)
        parts[grp] = term[lax.rem(grp, 2), rows, cols]

    settle(len(BACK) - 1)
    all_parts(lambda copy: copy.wait_recv())
    share[...] = jnp.sum(parts[...].astype(F32), axis=0)
    to_seq(lambda to: wg_copy(to).start())
    wg_in[seq] = share[...]

    for copy in rings:
        copy.wait_send()
    for slot in range(len(OFFSETS)):
        core_copy(slot).wait_send()
    for c in range(len(THERE)):
        all_halo(c).wait_send()
    all_aq().wait_send()
    all_hg(len(BACK) - 1).wait_send()
    all_parts(lambda copy: copy.wait_send())
    all_wg().wait_send()
    all_wg().wait_recv()
    for piece in range(n_seq):
        rows, cols = corner(piece)
        wg_out[rows, cols] = wg_in[piece]
    for c in range(len(BACK)):
        all_dkv(c).wait_send()
    for c in range(len(BACK)):
        all_dkv(c).wait_recv()
    for store in stores:
        store.wait()


def layer(send, lists, counts, q, k, v, cot, weight, n_seq, n_grp):
    rows, width = q.shape
    tile = (rows, LANES)
    per_group = width // n_grp
    space = n_seq + n_grp
    items = lists.shape[1] * lists.shape[2]
    dma = pltpu.SemaphoreType.DMA
    inverse_root = 1.0 / math.sqrt(float(rows * n_seq * n_grp))
    return pl.pallas_call(
        functools.partial(layer_kernel, inverse_root),
        in_specs=[SMEM] * 3 + [ANY] * 5,
        out_specs=(ANY, ANY, ANY, VMEM),
        out_shape=(
            shape(q.shape),
            shape(q.shape),
            shape((n_seq,) + tile),
            shape((per_group, width), F32),
        ),
        scratch_shapes=[pltpu.VMEM(q.shape, BF)] * 4
        + [
            pltpu.VMEM(weight.shape, BF),
            pltpu.VMEM((n_seq,) + tile, BF),
            [pltpu.VMEM((n_seq, size, LANES), BF) for size in THERE],
            pltpu.VMEM((n_seq,) + tile, BF),
            pltpu.VMEM((n_seq,) + tile, BF),
            [pltpu.VMEM((n_grp, size, LANES), BF) for size in THERE],
            pltpu.VMEM((space,) + tile, BF),
            pltpu.VMEM((space, LANES, rows), BF),
            pltpu.VMEM((n_seq, 2 * rows, LANES), BF),
            pltpu.VMEM((items,) + tile, F32),
            pltpu.VMEM((items,) + tile, F32),
            pltpu.VMEM((n_seq,) + tile, BF),
            pltpu.VMEM((n_seq,) + tile, BF),
            pltpu.VMEM((n_seq, HD, rows), BF),
            pltpu.VMEM(q.shape, BF),
            pltpu.VMEM((n_seq,) + tile, F32),
            pltpu.VMEM((n_grp,) + tile, BF),
            [pltpu.VMEM((n_grp, size, LANES), BF) for size in BACK],
            [pltpu.VMEM((n_grp, size, LANES), F32) for size in BACK],
            [pltpu.VMEM((n_seq, size, LANES), BF) for size in BACK],
            pltpu.VMEM((len(OFFSETS), 2) + cot.shape, BF),
            pltpu.VMEM((HD, width), F32),
            pltpu.VMEM((2, per_group, width), BF),
            pltpu.VMEM((n_grp, per_group // 2, LANES), BF),
            pltpu.VMEM((per_group // 2, LANES), F32),
            pltpu.VMEM((n_seq, per_group // 2, LANES), F32),
            pltpu.VMEM((items, items), jnp.int32),
            pltpu.VMEM((8, items), jnp.int32),
            pltpu.SMEM((8, items), jnp.int32),
            dma((6,)),
            dma((2 + len(BACK),)),
            dma((8,)),
            dma((8,)),
            dma((len(OFFSETS),)),
            dma((len(OFFSETS),)),
            dma((len(THERE),)),
            dma((len(THERE),)),
            dma,
            dma,
            dma((len(THERE),)),
            dma((len(THERE),)),
            dma,
            dma,
            dma((len(BACK),)),
            dma((len(BACK),)),
            dma((len(BACK),)),
            dma((len(BACK),)),
            dma,
            dma,
            dma,
            dma,
        ],
        compiler_params=pltpu.CompilerParams(
            vmem_limit_bytes=LIMIT, collective_id=0, has_side_effects=True
        ),
    )(send, lists, counts, q, k, v, cot, weight)


def finish_kernel(out_in, dq_in, kv_ref, wg_in, out_ref, dq_ref, dk_ref, dv_ref, wg_ref):
    out_ref[...] = out_in[...]
    dq_ref[...] = dq_in[...]
    wg_ref[...] = wg_in[...]
    for j in range(kv_ref.shape[0] // 2):
        cols = slice(j * LANES, (j + 1) * LANES)
        first, second = weave(kv_ref[2 * j], kv_ref[2 * j + 1])
        dk_ref[:, cols] = first.astype(BF)
        dv_ref[:, cols] = second.astype(BF)


def per_device(
    queries, key_rows, value_rows, cotangent, out_weight, send_lists, key_blocks, key_counts
):
    send = send_lists.transpose(0, 2, 1)
    lists = key_blocks.transpose(0, 2, 1)
    out, dq, dkv, weight_grad = layer(
        send,
        lists,
        key_counts,
        queries,
        key_rows,
        value_rows,
        cotangent,
        out_weight,
        lax.axis_size("seq"),
        lax.axis_size("grp"),
    )
    flat = shape(queries.shape)
    return pl.pallas_call(
        finish_kernel,
        in_specs=[VMEM] * 4,
        out_specs=(VMEM,) * 5,
        out_shape=(flat,) * 4 + (shape(weight_grad.shape, F32),),
        compiler_params=pltpu.CompilerParams(vmem_limit_bytes=LIMIT),
    )(out, dq, dkv, weight_grad)


def solution(mesh):
    nodes = P(("seq", "grp"), None)
    by_group = P("grp", None, None)
    return jax.shard_map(
        per_device,
        mesh=mesh,
        in_specs=(nodes, nodes, nodes, nodes, P(), by_group, by_group, P("grp", None)),
        out_specs=(nodes, nodes, nodes, nodes, P("grp", None)),
        check_vma=False,
    )
```

```python
import functools
import math

import jax
import jax.numpy as jnp
from jax import lax
from jax.experimental import pallas as pl
from jax.experimental.pallas import tpu as pltpu
from jax.sharding import PartitionSpec as P

HD = 64
LANES = 128
BF = jnp.bfloat16
F32 = jnp.float32
VMEM = pl.BlockSpec(memory_space=pltpu.VMEM)
SMEM = pl.BlockSpec(memory_space=pltpu.SMEM)
ANY = pl.BlockSpec(memory_space=pl.ANY)
LIMIT = 60 * 1024 * 1024
THERE = (64, 64)
BACK = (64, 64)
MESH = pl.DeviceIdType.MESH


def weave(left, right):
    lane = lax.broadcasted_iota(jnp.int32, left.shape, 1)
    left_f, right_f = left.astype(F32), right.astype(F32)
    first = jnp.where(lane < HD, left_f, pltpu.roll(right_f, HD, 1))
    second = jnp.where(lane < HD, pltpu.roll(left_f, HD, 1), right_f)
    return first, second


def shape(dims, kind=BF):
    return jax.ShapeDtypeStruct(dims, kind)


def signal(semaphore, seq, grp):
    pl.semaphore_signal(semaphore, inc=1, device_id=(seq, grp), device_id_type=MESH)


def others(count, body):
    def step(k, carry):
        body(k)
        return carry

    lax.fori_loop(1, count, step, 0)


def each(count, body, unroll=1):
    def step(i, carry):
        body(i)
        return carry

    lax.fori_loop(0, count, step, 0, unroll=unroll)


def push(src, dst, send, recv, seq, grp):
    return pltpu.make_async_remote_copy(
        src_ref=src,
        dst_ref=dst,
        send_sem=send,
        recv_sem=recv,
        device_id=(seq, grp),
        device_id_type=MESH,
    )


def local(src, dst, semaphore):
    return pltpu.make_async_copy(src, dst, semaphore)


def span_of(sizes, c):
    return slice(sum(sizes[:c]), sum(sizes[: c + 1]))


def rows_of(ref, block, sizes, c):
    return ref.at[block, pl.ds(sum(sizes[:c]), sizes[c])]


def place_order(place):
    row = lax.broadcasted_iota(jnp.int32, place.shape, 0)
    col = lax.broadcasted_iota(jnp.int32, place.shape, 1)
    other = place.T
    earlier = (other < place) | ((other == place) & (col < row))
    rank = jnp.sum(jnp.where(earlier, 1, 0), axis=1, keepdims=True)
    there = rank == col

    def down(mask, value):
        return jnp.sum(jnp.where(mask, value, 0), axis=0, keepdims=True)

    order = down(there, row)
    sorted_place = down(there, place)
    again = (sorted_place == pltpu.roll(sorted_place, 1, 1)) & (col[:1] > 0)
    last = jnp.maximum(down(place <= col, 1) - 1, 0)
    return jnp.concatenate((order, jnp.where(again, 1, 0), last, down(place == col, 1)), axis=0)


def make_plan(send_ref, list_ref, place, plan):
    listed, blocks = list_ref.shape[1:]
    groups = send_ref.shape[2]

    def put(i, value):
        place[pl.ds(i, 1), :] = jnp.full((1, place.shape[1]), value, jnp.int32)

    def pairs(b):
        for t in range(listed):
            put(b * listed + t, list_ref[0, t, b])

    each(blocks, pairs)
    for_pairs = place_order(place[...])
    place[...] = jnp.full(place.shape, place.shape[1], jnp.int32)
    each(groups, lambda g: put(g, send_ref[0, 0, g]))
    plan[...] = jnp.concatenate((for_pairs, place_order(place[...])), axis=0)


def split_pair(pair):
    lane = lax.broadcasted_iota(jnp.int32, pair.shape, 1)
    full = pair.astype(F32)
    scale = 1.0 / math.sqrt(HD)
    return jnp.concatenate(
        (
            jnp.where(lane < HD, full * scale, 0.0).astype(BF),
            jnp.where(lane < HD, 0.0, full).astype(BF),
        ),
        axis=0,
    )


def attend_blocks(blocks, list_ref, count_ref, x_ref, kv_ref, kv_t, aq_ref, att_t, terms):
    listed = list_ref.shape[1]
    rows = kv_ref.shape[1]
    scale = 1.0 / math.sqrt(HD)
    span = range(listed)
    index = [[list_ref[0, t, b] for t in span] for b in blocks]
    xs = [x_ref[b] for b in blocks]
    both = [
        lax.dot_general(
            jnp.concatenate([kv_ref[i] for i in at], axis=0),
            x,
            (((1,), (1,)), ((), ())),
            preferred_element_type=F32,
        )
        for at, x in zip(index, xs)
    ]
    zs = []
    for b, pair in zip(blocks, both):
        bias = [jnp.where(count_ref[0, b] > t, 0.0, -jnp.inf).astype(F32) for t in span]
        scores = [pair[t * rows : (t + 1) * rows, :rows] + bias[t] for t in span]
        dprobs = [pair[t * rows : (t + 1) * rows, rows:] for t in span]
        top = functools.reduce(jnp.maximum, scores)
        top = jnp.max(top, axis=0, keepdims=True)
        weights = [jnp.exp(s - top) for s in scores]
        inverse = 1.0 / jnp.sum(sum(weights), axis=0, keepdims=True)
        inner = sum(w * d for w, d in zip(weights, dprobs))
        inner = jnp.sum(inner, axis=0, keepdims=True) * inverse
        z = []
        for w, d in zip(weights, dprobs):
            probs = w * inverse
            z.append(jnp.concatenate((probs * (d - inner), probs), axis=1).astype(BF))
        zs.append(z)
    for b, z, x in zip(blocks, zs, xs):
        pair = jnp.dot(jnp.concatenate(z, axis=0), x, preferred_element_type=F32)
        for t in span:
            terms[b * listed + t] = pair[t * rows : (t + 1) * rows]
    for b, z, at in zip(blocks, zs, index):
        turned = jnp.concatenate([kv_t[i] for i in at], axis=1)
        out = jnp.dot(turned, jnp.concatenate(z, axis=0), preferred_element_type=F32)
        attended = out[HD:, rows:]
        att_t[b] = attended.astype(BF)
        aq_ref[b] = jnp.concatenate((out[:HD, :rows] * scale, attended), axis=0).T.astype(BF)


def sums_by_place(plan_ref, at, source, running, span=slice(None)):
    def run(j, total):
        total = jnp.where(plan_ref[at + 1, j] != 0, total, 0.0)
        total = total + source[plan_ref[at, j], span].astype(F32)
        running[j, span] = total
        return total

    rows = len(range(*span.indices(running.shape[1])))
    zero = jnp.zeros((rows, running.shape[2]), F32)
    lax.fori_loop(0, running.shape[0], run, zero, unroll=4)


def sum_of(place, plan_ref, at, running, span=slice(None)):
    return jnp.where(plan_ref[at + 3, place] != 0, running[plan_ref[at + 2, place], span], 0.0)


OFFSETS = (0, -1, 1, -2, 2, -3, 3, 4)
SIDE = 4


def layer_kernel(
    inverse_root,
    send_ref,
    list_ref,
    count_ref,
    q_hbm,
    k_hbm,
    v_hbm,
    c_hbm,
    w_hbm,
    out_hbm,
    dq_hbm,
    kv_back,
    wg_out,
    q_ref,
    k_ref,
    v_ref,
    c_ref,
    w_ref,
    kv_out,
    kv_in,
    qg_out,
    qg_in,
    halo_out,
    kv_ref,
    kv_t,
    x_ref,
    terms,
    running,
    aq_out,
    aq_in,
    att_t,
    att_n,
    own_grad,
    halo_grad,
    back,
    back_sum,
    dkv,
    cot_ref,
    total,
    term,
    parts,
    share,
    wg_in,
    place,
    plan,
    plan_ref,
    load_sem,
    local_sem,
    ring_send,
    ring_recv,
    core_send,
    core_recv,
    kv_send,
    kv_recv,
    qg_send,
    qg_recv,
    halo_send,
    halo_recv,
    aq_send,
    aq_recv,
    hg_send,
    hg_recv,
    dkv_send,
    dkv_recv,
    part_send,
    part_recv,
    wg_send,
    wg_recv,
):
    seq, grp = lax.axis_index("seq"), lax.axis_index("grp")
    n_seq, n_grp = qg_in.shape[0], halo_grad.shape[0]
    half = wg_out.shape[0] // 2
    middle = cot_ref.shape[2] // 2
    right, left = lax.rem(seq + 2, n_seq), lax.rem(seq + n_seq - 2, n_seq)
    core = lax.rem(seq, 2)
    sibling = seq + 1 - 2 * core
    next_grp = lax.rem(grp + 1, n_grp)
    source = grp // 2
    keeps_one = source == seq
    tiles = [slice(j * LANES, (j + 1) * LANES) for j in range(n_seq // 2)]

    pairs = ((k_hbm, k_ref), (v_hbm, v_ref), (c_hbm, c_ref), (w_hbm, w_ref), (q_hbm, q_ref))
    loads = [local(src, dst, load_sem.at[i]) for i, (src, dst) in enumerate(pairs)]
    for load in loads:
        load.start()
    barrier = pltpu.get_barrier_semaphore()
    others(n_seq, lambda k: signal(barrier, lax.rem(seq + k, n_seq), grp))
    others(n_grp, lambda k: signal(barrier, seq, lax.rem(grp + k, n_grp)))

    def greet(g):
        pl.when((source != seq) | (g != grp))(lambda: signal(barrier, source, g))

    each(n_grp, greet)

    most, rest = pl.ds(0, n_seq - 1), pl.ds(0, n_grp - 1)

    def kv_copy(c, to, src=None, dst=None):
        src = rows_of(kv_out, to, THERE, c) if src is None else src
        dst = kv_in[c].at[seq] if dst is None else dst
        return push(src, dst, kv_send.at[c], kv_recv.at[c], to, grp)

    def all_kv(c):
        src = rows_of(kv_out, most, THERE, c)
        return kv_copy(c, sibling, src, kv_in[c].at[most])

    def qg_copy(to, src=None, dst=None):
        src = qg_out.at[to] if src is None else src
        dst = qg_in.at[seq] if dst is None else dst
        return push(src, dst, qg_send, qg_recv, to, grp)

    def all_qg():
        return qg_copy(sibling, qg_out.at[most], qg_in.at[most])

    def halo_copy(c, to, src=None, dst=None):
        src = halo_out[c].at[to] if src is None else src
        dst = rows_of(kv_ref, n_seq + grp, THERE, c) if dst is None else dst
        return push(src, dst, halo_send.at[c], halo_recv.at[c], seq, to)

    def all_halo(c):
        dst = rows_of(kv_ref, pl.ds(n_seq, n_grp - 1), THERE, c)
        return halo_copy(c, next_grp, halo_out[c].at[rest], dst)

    def aq_copy(to, src=None, dst=None):
        src = aq_out.at[to] if src is None else src
        dst = aq_in.at[seq] if dst is None else dst
        return push(src, dst, aq_send, aq_recv, to, grp)

    def all_aq():
        return aq_copy(sibling, aq_out.at[most], aq_in.at[most])

    def hg_copy(c, to, src=None, dst=None):
        src = rows_of(halo_grad, to, BACK, c) if src is None else src
        dst = back[c].at[grp] if dst is None else dst
        return push(src, dst, hg_send.at[c], hg_recv.at[c], seq, to)

    def all_hg(c):
        return hg_copy(c, next_grp, rows_of(halo_grad, rest, BACK, c), back[c].at[rest])

    def dkv_copy(c, to, src=None, dst=None):
        src = dkv[c].at[to] if src is None else src
        dst = rows_of(kv_back, seq, BACK, c) if dst is None else dst
        return push(src, dst, dkv_send.at[c], dkv_recv.at[c], to, grp)

    def all_dkv(c):
        return dkv_copy(c, sibling, dkv[c].at[most], rows_of(kv_back, most, BACK, c))

    def to_seq(body):
        others(n_seq, lambda k: body(lax.rem(seq + k, n_seq)))

    def to_grp(body):
        others(n_grp, lambda k: body(lax.rem(grp + k, n_grp)))

    def ring_copy(i, src, dst):
        to = right if i % 2 == 0 else left
        return push(src, dst, ring_send.at[i], ring_recv.at[i], to, grp)

    def core_copy(slot):
        return push(
            cot_ref.at[slot, 0],
            cot_ref.at[slot, 1],
            core_send.at[slot],
            core_recv.at[slot],
            sibling,
            grp,
        )

    def corner(piece):
        return (
            pl.ds(pl.multiple_of((piece % 2) * half, half), half),
            pl.ds(pl.multiple_of((piece // 2) * LANES, LANES), LANES),
        )

    def part_copy(row, piece):
        rows, cols = corner(piece)
        return push(
            term.at[row, rows, cols], parts.at[grp], part_send, part_recv, piece, 2 * seq + row
        )

    def all_parts(body):
        for mine in (0, 1):
            every = parts.at[pl.ds(0, n_grp - mine)]
            copy = push(every, every, part_send, part_recv, sibling, grp)
            pl.when(keeps_one if mine else jnp.logical_not(keeps_one))(functools.partial(body, copy))

    def each_part(body):
        for row in range(2):

            def step(piece, row=row):
                elsewhere = (piece != seq) | (2 * seq + row != grp)
                pl.when(elsewhere)(lambda: body(row, piece))

            each(n_seq, step)

    def wg_copy(to):
        return push(share, wg_in.at[seq], wg_send, wg_recv, to, grp)

    def all_wg():
        return push(wg_in.at[most], wg_in.at[most], wg_send, wg_recv, sibling, grp)

    loads[0].wait()
    loads[1].wait()
    for j, cols in enumerate(tiles):
        first, second = weave(k_ref[:, cols], v_ref[:, cols])
        kv_out[2 * j] = first.astype(BF)
        kv_out[2 * j + 1] = second.astype(BF)
    pl.semaphore_wait(barrier, n_seq + n_grp - 2 + 2 * n_seq - jnp.where(keeps_one, 1, 0))
    to_seq(lambda to: kv_copy(0, to).start())
    for load in loads[2:]:
        load.wait()
    grad = lax.dot_general(
        c_ref[...], w_ref[...], (((1,), (1,)), ((), ())), preferred_element_type=F32
    ).astype(BF)
    for j, cols in enumerate(tiles):
        first, second = weave(q_ref[:, cols], grad[:, cols])
        qg_out[2 * j] = first.astype(BF)
        qg_out[2 * j + 1] = second.astype(BF)
    cot_ref[0, 0] = c_ref[...]
    qg_in[seq] = qg_out[seq]
    def pass_on(c):
        mine, span = kv_in[c], span_of(THERE, c)
        mine[seq] = kv_out[seq, span]
        all_kv(c).wait_recv()

        def forward(to):
            halo_out[c][to] = mine[send_ref[0, 0, to]]
            halo_copy(c, to).start()

        to_grp(forward)
        kv_ref[n_seq + grp, span] = mine[send_ref[0, 0, grp]]
        kv_ref[:n_seq, span] = mine[...]

    for c in range(1, len(THERE)):
        all_kv(c - 1).wait_send()
        to_seq(lambda to, c=c: kv_copy(c, to).start())
        pass_on(c - 1)
    all_kv(len(THERE) - 1).wait_send()
    to_seq(lambda to: qg_copy(to).start())
    pass_on(len(THERE) - 1)

    def turn(i):
        kv_t[i] = kv_ref[i].T

    each(n_seq, turn, 4)
    make_plan(send_ref, list_ref, place, plan)
    plan_load = local(plan, plan_ref, load_sem.at[5])
    plan_load.start()
    all_qg().wait_send()
    rings = [ring_copy(0, cot_ref.at[0, 0], cot_ref.at[1, 0])]
    rings.append(ring_copy(1, cot_ref.at[0, 0], cot_ref.at[2, 0]))
    for copy in rings:
        copy.start()
    core_copy(0).start()
    all_qg().wait_recv()

    def prepare(b):
        x_ref[b] = split_pair(qg_in[b])

    each(n_seq, prepare, 2)
    for c in range(len(THERE)):
        all_halo(c).wait_recv()
    each(n_grp, lambda g: turn(n_seq + g), 4)
    for i in range(2, 6):
        rings.append(ring_copy(i, cot_ref.at[i - 1, 0], cot_ref.at[i + 1, 0]))

    def ring_step(first):
        for way in range(2):
            rings[first + way].wait_recv()
            rings[first + 2 + way].start()
            core_copy(first + 1 + way).start()

    plan_load.wait()

    def step(i):
        blocks = [i * SIDE + j for j in range(SIDE)]
        attend_blocks(
            blocks, list_ref, count_ref, x_ref, kv_ref, kv_t, aq_out, att_t, terms
        )
        for b in blocks:
            pl.when(b != seq)(aq_copy(b).start)
        pl.when(i == 0)(lambda: ring_step(0))

    each(n_seq // SIDE, step)
    aq_in[seq] = aq_out[seq]

    def sum_up(c):
        sums_by_place(plan_ref, 0, terms, running, span_of(BACK, c))

    def give(c, to):
        span = span_of(BACK, c)
        halo_grad[to, span] = sum_of(n_seq + to, plan_ref, 0, running, span).astype(BF)
        hg_copy(c, to).start()

    sum_up(0)
    to_grp(functools.partial(give, 0))
    ring_step(2)
    for c in range(1, len(BACK)):
        sum_up(c)
    mine = sum_of(n_seq + grp, plan_ref, 0, running).astype(BF)
    for c in range(len(BACK)):
        back[c][grp] = mine[span_of(BACK, c)]

    def keep(b):
        own_grad[b] = sum_of(b, plan_ref, 0, running)

    each(n_seq, keep, 4)

    def block_of(offset, of_core):
        return lax.rem(seq - core + 2 * offset + n_seq, n_seq) + of_core

    def add(slot):
        core_copy(slot).wait_recv()
        att = jnp.concatenate(
            (att_t[block_of(OFFSETS[slot], core)], att_t[block_of(OFFSETS[slot], 1 - core)]),
            axis=1,
        )
        cot = cot_ref[slot].reshape(att.shape[1], cot_ref.shape[3])
        part = jnp.dot(att, cot, preferred_element_type=F32) * inverse_root
        total[...] = part if slot == 0 else total[...] + part

    for slot in range(5):
        add(slot)
    for c in range(1, len(BACK)):
        all_hg(c - 1).wait_send()
        to_grp(functools.partial(give, c))
    for way in range(2):
        rings[4 + way].wait_recv()
        where = pl.ds(way * middle, middle)
        rings.append(ring_copy(6 + way, cot_ref.at[5 + way, 0, where], cot_ref.at[7, 0, where]))
        rings[-1].start()
        core_copy(5 + way).start()

    stores = []

    def settle(c):
        span = span_of(BACK, c)
        all_hg(c).wait_recv()
        sums_by_place(plan_ref, 4, back[c], back_sum[c])

        def finish(b):
            more = sum_of(b, plan_ref, 4, back_sum[c])
            dkv[c][b] = (own_grad[b, span] + more).astype(BF)

        each(n_seq, finish, 4)
        to_seq(lambda to: dkv_copy(c, to).start())
        stores.append(local(dkv[c].at[seq], rows_of(kv_back, seq, BACK, c), local_sem.at[2 + c]))
        stores[-1].start()

    for c in range(len(BACK) - 1):
        settle(c)

    all_aq().wait_recv()
    for j, cols in enumerate(tiles):
        first, second = weave(aq_in[2 * j], aq_in[2 * j + 1])
        q_ref[:, cols] = first.astype(BF)
        att_n[:, cols] = second.astype(BF)
    k_ref[...] = jnp.dot(att_n[...], w_ref[...], preferred_element_type=F32).astype(BF)
    for store in (local(q_ref, dq_hbm, local_sem.at[0]), local(k_ref, out_hbm, local_sem.at[1])):
        store.start()
        stores.append(store)
    for slot in range(5, 7):
        add(slot)

    for way in range(2):
        rings[6 + way].wait_recv()
    core_copy(7).start()
    add(7)
    for row in range(2):
        term[row] = total[2 * half * row : 2 * half * (row + 1)].astype(BF)
    each_part(lambda row, piece: part_copy(row, piece).start())

    @pl.when(keeps_one)
    def _():
        rows, cols = corner(seq)
        parts[grp] = term[lax.rem(grp, 2), rows, cols]

    settle(len(BACK) - 1)
    all_parts(lambda copy: copy.wait_recv())
    share[...] = jnp.sum(parts[...].astype(F32), axis=0)
    to_seq(lambda to: wg_copy(to).start())
    wg_in[seq] = share[...]

    for copy in rings:
        copy.wait_send()
    for slot in range(len(OFFSETS)):
        core_copy(slot).wait_send()
    for c in range(len(THERE)):
        all_halo(c).wait_send()
    all_aq().wait_send()
    all_hg(len(BACK) - 1).wait_send()
    all_parts(lambda copy: copy.wait_send())
    all_wg().wait_send()
    all_wg().wait_recv()
    for piece in range(n_seq):
        rows, cols = corner(piece)
        wg_out[rows, cols] = wg_in[piece]
    for c in range(len(BACK)):
        all_dkv(c).wait_send()
    for c in range(len(BACK)):
        all_dkv(c).wait_recv()
    for store in stores:
        store.wait()


def layer(send, lists, counts, q, k, v, cot, weight, n_seq, n_grp):
    rows, width = q.shape
    tile = (rows, LANES)
    per_group = width // n_grp
    space = n_seq + n_grp
    items = lists.shape[1] * lists.shape[2]
    dma = pltpu.SemaphoreType.DMA
    inverse_root = 1.0 / math.sqrt(float(rows * n_seq * n_grp))
    return pl.pallas_call(
        functools.partial(layer_kernel, inverse_root),
        in_specs=[SMEM] * 3 + [ANY] * 5,
        out_specs=(ANY, ANY, ANY, VMEM),
        out_shape=(
            shape(q.shape),
            shape(q.shape),
            shape((n_seq,) + tile),
            shape((per_group, width), F32),
        ),
        scratch_shapes=[pltpu.VMEM(q.shape, BF)] * 4
        + [
            pltpu.VMEM(weight.shape, BF),
            pltpu.VMEM((n_seq,) + tile, BF),
            [pltpu.VMEM((n_seq, size, LANES), BF) for size in THERE],
            pltpu.VMEM((n_seq,) + tile, BF),
            pltpu.VMEM((n_seq,) + tile, BF),
            [pltpu.VMEM((n_grp, size, LANES), BF) for size in THERE],
            pltpu.VMEM((space,) + tile, BF),
            pltpu.VMEM((space, LANES, rows), BF),
            pltpu.VMEM((n_seq, 2 * rows, LANES), BF),
            pltpu.VMEM((items,) + tile, F32),
            pltpu.VMEM((items,) + tile, F32),
            pltpu.VMEM((n_seq,) + tile, BF),
            pltpu.VMEM((n_seq,) + tile, BF),
            pltpu.VMEM((n_seq, HD, rows), BF),
            pltpu.VMEM(q.shape, BF),
            pltpu.VMEM((n_seq,) + tile, F32),
            pltpu.VMEM((n_grp,) + tile, BF),
            [pltpu.VMEM((n_grp, size, LANES), BF) for size in BACK],
            [pltpu.VMEM((n_grp, size, LANES), F32) for size in BACK],
            [pltpu.VMEM((n_seq, size, LANES), BF) for size in BACK],
            pltpu.VMEM((len(OFFSETS), 2) + cot.shape, BF),
            pltpu.VMEM((HD, width), F32),
            pltpu.VMEM((2, per_group, width), BF),
            pltpu.VMEM((n_grp, per_group // 2, LANES), BF),
            pltpu.VMEM((per_group // 2, LANES), F32),
            pltpu.VMEM((n_seq, per_group // 2, LANES), F32),
            pltpu.VMEM((items, items), jnp.int32),
            pltpu.VMEM((8, items), jnp.int32),
            pltpu.SMEM((8, items), jnp.int32),
            dma((6,)),
            dma((2 + len(BACK),)),
            dma((8,)),
            dma((8,)),
            dma((len(OFFSETS),)),
            dma((len(OFFSETS),)),
            dma((len(THERE),)),
            dma((len(THERE),)),
            dma,
            dma,
            dma((len(THERE),)),
            dma((len(THERE),)),
            dma,
            dma,
            dma((len(BACK),)),
            dma((len(BACK),)),
            dma((len(BACK),)),
            dma((len(BACK),)),
            dma,
            dma,
            dma,
            dma,
        ],
        compiler_params=pltpu.CompilerParams(
            vmem_limit_bytes=LIMIT, collective_id=0, has_side_effects=True
        ),
    )(send, lists, counts, q, k, v, cot, weight)


def finish_kernel(out_in, dq_in, kv_ref, wg_in, out_ref, dq_ref, dk_ref, dv_ref, wg_ref):
    out_ref[...] = out_in[...]
    dq_ref[...] = dq_in[...]
    wg_ref[...] = wg_in[...]
    for j in range(kv_ref.shape[0] // 2):
        cols = slice(j * LANES, (j + 1) * LANES)
        first, second = weave(kv_ref[2 * j], kv_ref[2 * j + 1])
        dk_ref[:, cols] = first.astype(BF)
        dv_ref[:, cols] = second.astype(BF)


def per_device(
    queries, key_rows, value_rows, cotangent, out_weight, send_lists, key_blocks, key_counts
):
    send = send_lists.transpose(0, 2, 1)
    lists = key_blocks.transpose(0, 2, 1)
    out, dq, dkv, weight_grad = layer(
        send,
        lists,
        key_counts,
        queries,
        key_rows,
        value_rows,
        cotangent,
        out_weight,
        lax.axis_size("seq"),
        lax.axis_size("grp"),
    )
    flat = shape(queries.shape)
    return pl.pallas_call(
        finish_kernel,
        in_specs=[VMEM] * 4,
        out_specs=(VMEM,) * 5,
        out_shape=(flat,) * 4 + (shape(weight_grad.shape, F32),),
        compiler_params=pltpu.CompilerParams(vmem_limit_bytes=LIMIT),
    )(out, dq, dkv, weight_grad)


def solution(mesh):
    nodes = P(("seq", "grp"), None)
    by_group = P("grp", None, None)
    return jax.shard_map(
        per_device,
        mesh=mesh,
        in_specs=(nodes, nodes, nodes, nodes, P(), by_group, by_group, P("grp", None)),
        out_specs=(nodes, nodes, nodes, nodes, P("grp", None)),
        check_vma=False,
    )
```
